32 devices in a mesh: sky: 8 (over z, x), depth: 4 (over y, core).
Axes of the slice: x: 2, y: 2, z: 4, core: 2. Of those that a mesh axis runs over, the one named last changes fastest.
Arguments:
- positions: float32 [3, 512, 128], P(None, ('sky', 'depth')), may hold values from 0 to 1
- cell_points: int32 [512], P(('sky', 'depth')), may hold values from 1 to 128
- target_log: float32 [16], replicated, may hold values from 8 to 20
- export_count: int32 [32, 32], P(('sky', 'depth')), may hold values from 0 to 3, as said below
- export_cell: int32 [32, 32, 3], P(('sky', 'depth')), may hold values from 0 to 15
- import_pair: int32 [32, 32, 3], P(('sky', 'depth')), may hold values from 0 to 15
- import_shift: int32 [3, 32, 32, 3], P(None, ('sky', 'depth')), may hold values from -1 to 1, as said below
Outputs:
- travel: float32 [3, 512, 128], P(None, ('sky', 'depth'))
The draws below stay inside these ranges and needn't reach their ends.
Inputs may be any that keep to these rules, and one draw needn't show every extreme that they name: export_count[s, t] counts the slots of export_cell[s, t] that are used; it is zero unless s and t are distinct devices whose sky indices differ by at most one modulo the sky axis's size and whose depth indices differ by at most one; in every draw some device t receives 3 cells from each such neighbour. For neighbouring devices t and s, components 0 and 2 of import_shift[:, t, s, k] are the sky step and the depth step from t's region to s's region (sky taken around the cycle), component 1 varies; all components are zero for devices that are not neighbours.
All inputs are finite; a program needn't handle non-finite values.
Results may differ from the reference program's by a relative error of at most 0.00022.
Values sent between devices are 32-bit elements; how exact they have to be, the bound alone decides.
A program may use at most 64 MiB of HBM per device.

```python
import jax
import jax.numpy as jnp
from jax import lax

PTS = 128
BINS = 16
SLOTS = 3
STEPS = 2
CELL_DEV = 16
PEERS = 32
CELLS = 512
N_SKY = 8
N_DEPTH = 4


def region_steps():
    device_ids = jnp.arange(PEERS, dtype=jnp.int32)
    sky_ids = device_ids // N_DEPTH
    depth_ids = device_ids % N_DEPTH
    sky_step = (sky_ids[None, :] - sky_ids[:, None] + 1) % N_SKY - 1
    depth_step = depth_ids[None, :] - depth_ids[:, None]
    near = (jnp.abs(sky_step) <= 1) & (jnp.abs(depth_step) <= 1) & (device_ids[None, :] != device_ids[:, None])
    return (sky_step, depth_step, near)


def draw_export_count(key, part):
    sky_step, depth_step, near = region_steps()
    base_counts = jax.random.randint(key, (PEERS, PEERS), 0, SLOTS + 1)
    busiest = jax.random.randint(jax.random.fold_in(key, 7), (), 0, PEERS)
    column = jnp.arange(PEERS)[None, :] == busiest
    filled = jnp.where(column, SLOTS, base_counts)
    return jnp.where(near, filled, 0).astype(jnp.int32)


def draw_import_shift(key, part):
    sky_step, depth_step, near = region_steps()
    across = jax.random.randint(key, (PEERS, PEERS, SLOTS), -1, 2)
    first = jnp.broadcast_to(sky_step[:, :, None], (PEERS, PEERS, SLOTS))
    third = jnp.broadcast_to(depth_step[:, :, None], (PEERS, PEERS, SLOTS))
    stacked = jnp.stack([first, across, third], axis=0)
    return jnp.where(near[None, :, :, None], stacked, 0).astype(jnp.int32)


def plant(values, rng, smallest, high):
    index_at = [jax.random.randint(jax.random.fold_in(rng, axis), (), 0, length) for axis, length in enumerate(values.shape)]
    widest = values.shape.index(max(values.shape))
    beside = index_at[:widest] + [(index_at[widest] + 1) % values.shape[widest]] + index_at[widest + 1:]
    return values.at[tuple(index_at)].set(smallest).at[tuple(beside)].set(high)


def levels(own_key, shape, cuts, smallest, high):
    gain = 1.0
    for position, blocks in cuts:
        heights = jax.random.uniform(jax.random.fold_in(jax.random.fold_in(own_key, 6), position), (blocks,), jnp.float32, smallest / len(cuts), high / len(cuts))
        gain = gain * jnp.repeat(jnp.exp(heights), shape[position] // blocks).reshape((-1,) + (1,) * (len(shape) - 1 - position))
    return gain


def setup_inputs(seed: int = 0) -> dict:
    key_list = jax.random.split(jax.random.key(seed), 8)
    positions = jnp.clip(1.0 * jax.random.uniform(key_list[0], (3, CELLS, PTS), jnp.float32) ** levels(key_list[0], (3, CELLS, PTS), ((1, 32),), -0.2, 0.2), 0.0, 1.0)
    cell_points = plant(jax.random.randint(key_list[1], (CELLS,), 1, PTS + 1), jax.random.fold_in(key_list[1], 1), 1, PTS).astype(jnp.int32)
    target_log = jnp.clip(jax.random.uniform(key_list[2], (BINS,), jnp.float32, 8.0, 20.0), 8.0, 20.0)
    export_count = draw_export_count(jax.random.fold_in(key_list[7], 71), 0)
    export_cell = plant(jax.random.randint(key_list[4], (PEERS, PEERS, SLOTS), 0, CELL_DEV), jax.random.fold_in(key_list[4], 1), 0, CELL_DEV - 1).astype(jnp.int32)
    import_pair = plant(jax.random.randint(key_list[5], (PEERS, PEERS, SLOTS), 0, CELL_DEV), jax.random.fold_in(key_list[5], 1), 0, CELL_DEV - 1).astype(jnp.int32)
    import_shift = draw_import_shift(jax.random.fold_in(key_list[7], 71), 0)
    return dict(positions=positions, cell_points=cell_points, target_log=target_log, export_count=export_count, export_cell=export_cell, import_pair=import_pair, import_shift=import_shift)


EPS_SQ = 0.0001
INV_WIDTH = 16.0
STEP_SIZE = 0.01

def pair_geometry(left_pos, left_mask, right_pos, right_mask, shifts, centres):
    offsets = left_pos[:, :, :, None] - right_pos[:, :, None, :] - shifts[:, :, None, None]
    radius = jnp.sqrt(lax.optimization_barrier(jnp.sum(offsets * offsets, axis=0)) + EPS_SQ)
    weight = left_mask[:, :, None] * right_mask[:, None, :]
    scaled = (radius[None] - centres[:, None, None, None]) * INV_WIDTH
    kernel = jnp.exp(-0.5 * scaled * scaled)
    return (offsets, radius, weight, scaled, kernel)

def block_counts(left_pos, left_mask, right_pos, right_mask, shifts, centres):
    offsets, radius, weight, scaled, kernel = pair_geometry(left_pos, left_mask, right_pos, right_mask, shifts, centres)
    return lax.optimization_barrier(jnp.sum(weight[None] * kernel, axis=(1, 2, 3)))

def block_forces(left_pos, left_mask, right_pos, right_mask, shifts, centres, bin_pull):
    offsets, radius, weight, scaled, kernel = pair_geometry(left_pos, left_mask, right_pos, right_mask, shifts, centres)
    slopes = lax.optimization_barrier(jnp.sum(bin_pull[:, None, None, None] * scaled * kernel, axis=0)) * -INV_WIDTH
    strength = weight * slopes / radius
    pulled = strength[None] * offsets
    return (lax.optimization_barrier(jnp.sum(pulled, axis=3)), -lax.optimization_barrier(jnp.sum(pulled, axis=2)))

def reference(positions, cell_points, target_log, export_count, export_cell, import_pair, import_shift):
    centres = (jnp.arange(BINS, dtype=jnp.float32) + 0.5) / INV_WIDTH
    point_mask = (jnp.arange(PTS, dtype=jnp.int32)[None, :] < cell_points[:, None]).astype(jnp.float32)
    dest_ids = jnp.broadcast_to(jnp.arange(PEERS, dtype=jnp.int32)[:, None, None], (PEERS, PEERS, SLOTS))
    source_ids = jnp.broadcast_to(jnp.arange(PEERS, dtype=jnp.int32)[None, :, None], (PEERS, PEERS, SLOTS))
    slot_ids = jnp.broadcast_to(jnp.arange(SLOTS, dtype=jnp.int32)[None, None, :], (PEERS, PEERS, SLOTS))
    sent_cells = jnp.transpose(export_cell, (1, 0, 2))
    sent_counts = jnp.transpose(export_count, (1, 0))[:, :, None]
    live_pairs = (slot_ids < sent_counts).astype(jnp.float32)
    block_rows = 64
    block_total = PEERS * PEERS * SLOTS // block_rows
    left_cells = (dest_ids * CELL_DEV + import_pair).astype(jnp.int32).reshape(block_total, block_rows)
    right_cells = (source_ids * CELL_DEV + sent_cells).astype(jnp.int32).reshape(block_total, block_rows)
    live_flat = live_pairs.reshape(block_total, block_rows)
    shift_flat = jnp.moveaxis(import_shift.astype(jnp.float32).reshape(3, block_total, block_rows), 1, 0)
    self_mask = point_mask.reshape(PEERS, CELL_DEV, PTS)
    zero_shift = jnp.zeros((3, CELL_DEV), jnp.float32)
    coords = positions
    travel = jnp.zeros_like(positions)
    for iteration in range(STEPS):
        self_pos = jnp.moveaxis(coords.reshape(3, PEERS, CELL_DEV, PTS), 1, 0)

        def self_count(running, item):
            cell_pos, cell_mask = item
            return (running + block_counts(cell_pos, cell_mask, cell_pos, cell_mask, zero_shift, centres), None)
        self_total, _ = lax.scan(self_count, jnp.zeros((BINS,), jnp.float32), (self_pos, self_mask))

        def ghost_count(running, item):
            left_ids, right_ids, live_now, shift_now = item
            part_sum = block_counts(coords[:, left_ids], point_mask[left_ids], coords[:, right_ids], point_mask[right_ids] * live_now[:, None], shift_now, centres)
            return (running + part_sum, None)
        ghost_total, _ = lax.scan(ghost_count, jnp.zeros((BINS,), jnp.float32), (left_cells, right_cells, live_flat, shift_flat))
        counts = 0.5 * self_total + ghost_total
        mean_count = jnp.mean(counts)
        bin_pull = (jnp.log(1.0 + counts) - target_log) * mean_count / (1.0 + counts)

        def self_force(item):
            cell_pos, cell_mask = item
            force_left, force_right = block_forces(cell_pos, cell_mask, cell_pos, cell_mask, zero_shift, centres, bin_pull)
            return force_left
        self_grad = lax.map(self_force, (self_pos, self_mask))
        gradient = jnp.moveaxis(self_grad, 0, 1).reshape(3, CELLS, PTS)

        def ghost_force(running, item):
            left_ids, right_ids, live_now, shift_now = item
            force_left, force_right = block_forces(coords[:, left_ids], point_mask[left_ids], coords[:, right_ids], point_mask[right_ids] * live_now[:, None], shift_now, centres, bin_pull)
            running = running.at[:, left_ids].add(force_left)
            running = running.at[:, right_ids].add(force_right)
            return (running, None)
        gradient, _ = lax.scan(ghost_force, gradient, (left_cells, right_cells, live_flat, shift_flat))
        power_sum = jnp.sum(gradient * gradient)
        valid_count = jnp.sum(point_mask)
        grad_rms = jnp.sqrt(power_sum / (3.0 * valid_count) + 1e-06)
        move_dir = -gradient / grad_rms
        travel = travel + move_dir
        coords = coords + STEP_SIZE * move_dir
    return travel
```

```python
import functools
import math

import jax
import jax.numpy as jnp
from jax import lax
from jax.experimental import pallas as pl
from jax.experimental.pallas import tpu as pltpu
from jax.sharding import PartitionSpec as P

STEPS = 2
EPS_SQ = 0.0001
INV_WIDTH = 16.0
STEP_SIZE = 0.01
FAR = 10000.0
LANES = 128
MESH = pl.DeviceIdType.MESH

LOG2E = math.log2(math.e)
HALF_ROOT = math.sqrt(0.5 * LOG2E)
GROUPS = ((7, 8), (12, 5), (15, 3))
REGIONS = [(a, b) for a in (-1, 0, 1) for b in (-1, 0, 1) if (a, b) != (0, 0)]


def bin_factor(anchor, k):
    return math.exp(sum(anchor - j - 8 for j in range(k)))


def geometry(left, right):
    offs = [left[i] - right[i] for i in range(3)]
    square = offs[0] * offs[0] + offs[1] * offs[1] + (offs[2] * offs[2] + EPS_SQ)
    inverse = lax.rsqrt(square)
    scaled = (square * inverse) * (INV_WIDTH * HALF_ROOT)
    anchors = []
    for anchor, _ in GROUPS:
        gap = scaled - HALF_ROOT * (anchor + 0.5)
        anchors.append(jnp.exp2(-(gap * gap)))
    ratio = jnp.exp2(8.0 * LOG2E - scaled * (LOG2E / HALF_ROOT))
    return offs, inverse, scaled, anchors, ratio


def fold(value):
    total = value[0:8]
    for start in range(8, value.shape[0], 8):
        total = total + value[start : start + 8]
    return total


def add_counts(sums, left, right):
    _, _, _, anchors, ratio = geometry(left, right)
    sums = list(sums)
    for (anchor, members), term in zip(GROUPS, anchors):
        for k in range(members):
            if k:
                term = term * ratio
            sums[anchor - k] = sums[anchor - k] + fold(term)
    return tuple(sums)


def pair_force(left, right, slope, extra):
    offs, inverse, scaled, anchors, ratio = geometry(left, right)
    radius16 = scaled * (1.0 / HALF_ROOT)
    first = None
    second = None
    for (anchor, members), term in zip(GROUPS, anchors):
        poly = slope(anchor - members + 1)
        poly_extra = extra(anchor - members + 1)
        for k in range(members - 2, -1, -1):
            poly = poly * ratio + slope(anchor - k)
            poly_extra = poly_extra * ratio + extra(anchor - k)
        poly = poly * term
        poly_extra = poly_extra * term
        first = poly if first is None else first + poly
        second = poly_extra if second is None else second + poly_extra
    strength = (radius16 * first - second) * inverse
    return [strength * off for off in offs]


def kernel(
    sky_count, depth_count, slots, unroll,
    pos_ref, points_ref, target_ref, ecount_ref, ecell_ref, ipair_ref, ishift_ref,
    out_ref,
    cl, cr, lg, rg, grad, work, coef, coef_x, row_grad,
    snd, rcv, ar_depth, ar_sky,
    snd_sem, rcv_sem, ard_send, ard_recv, ars_send, ars_recv,
):
    bins = 16
    cells = pos_ref.shape[1]
    ghosts = 8 * slots
    sky = lax.axis_index("sky")
    depth = lax.axis_index("depth")

    near = []
    for across, along in REGIONS:
        there_sky = lax.rem(sky + across + sky_count, sky_count)
        there_depth = depth + along
        clamped = jnp.clip(there_depth, 0, depth_count - 1)
        if along == 0:
            valid = None
        elif along < 0:
            valid = depth > 0
        else:
            valid = depth < depth_count - 1
        near.append((there_sky, clamped, there_sky * depth_count + clamped, valid))

    def when_valid(valid, action):
        if valid is None:
            action()
        else:
            pl.when(valid)(action)

    barrier = pltpu.get_barrier_semaphore()

    def greet(there_sky, there_depth):
        pl.semaphore_signal(barrier, inc=1, device_id=(there_sky, there_depth), device_id_type=MESH)

    for j in range(1, sky_count):
        greet(lax.rem(sky + j, sky_count), depth)
    for j in range(1, depth_count):
        greet(sky, lax.rem(depth + j, depth_count))
    for (across, along), (there_sky, there_depth, _, valid) in zip(REGIONS, near):
        if across != 0 and along != 0:
            when_valid(valid, functools.partial(greet, there_sky, there_depth))

    lane = lax.broadcasted_iota(jnp.int32, (1, LANES), 1)
    live_total = jnp.zeros((1, LANES), jnp.float32)
    for c in range(cells):
        live = lane < points_ref[c]
        live_total = live_total + jnp.where(live, 1.0, 0.0)
        x = pos_ref[0, c : c + 1, :]
        cl[0, c : c + 1, :] = jnp.where(live, x, FAR)
        cr[0, c : c + 1, :] = jnp.where(live, x, -FAR)
    for i in (1, 2):
        cl[i] = pos_ref[i]
        cr[i] = pos_ref[i]
    live_total = jnp.sum(live_total, axis=1, keepdims=True)

    for n in range(8):
        nid = near[n][2]
        for k in range(slots):
            cell = ecell_ref[0, nid, k]
            live = k < ecount_ref[0, nid]
            for i in range(3):
                row = cr[i, pl.ds(cell, 1), :]
                if i == 0:
                    row = jnp.where(live, row, -FAR)
                snd[0, n, i * slots + k : i * slots + k + 1, :] = row

    diagonals = 2 * jnp.where(depth > 0, 1, 0) + 2 * jnp.where(depth < depth_count - 1, 1, 0)
    pl.semaphore_wait(barrier, (sky_count - 1) + (depth_count - 1) + diagonals)

    def message(phase, n):
        there_sky, there_depth, _, _ = near[n]
        return pltpu.make_async_remote_copy(
            src_ref=snd.at[phase, n],
            dst_ref=rcv.at[phase, 7 - n],
            send_sem=snd_sem.at[phase, n],
            recv_sem=rcv_sem.at[phase, 7 - n],
            device_id=(there_sky, there_depth),
            device_id_type=MESH,
        )

    def arrival(phase, n):
        there_sky, there_depth, _, _ = near[n]
        return pltpu.make_async_remote_copy(
            src_ref=snd.at[phase, n],
            dst_ref=rcv.at[phase, n],
            send_sem=snd_sem.at[phase, n],
            recv_sem=rcv_sem.at[phase, n],
            device_id=(there_sky, there_depth),
            device_id_type=MESH,
        )

    def send_all(phase):
        for n in range(8):
            when_valid(near[n][3], lambda n=n: message(phase, n).start())

    def receive_all(phase):
        for n in range(8):
            when_valid(near[n][3], lambda n=n: arrival(phase, n).wait_recv())

    def drain_all(phase):
        for n in range(8):
            when_valid(near[n][3], lambda n=n: message(phase, n).wait_send())

    def reduce_stage(phase, row, buffer, send_sem, recv_sem, me, count, device):
        buffer[phase, me] = row

        def copy(j):
            peer = lax.rem(me + j, count)
            return pltpu.make_async_remote_copy(
                src_ref=buffer.at[phase, me],
                dst_ref=buffer.at[phase, me],
                send_sem=send_sem.at[phase, j],
                recv_sem=recv_sem.at[phase, me],
                device_id=device(peer),
                device_id_type=MESH,
            )

        for j in range(1, count):
            copy(j).start()
        for j in range(1, count):
            peer = lax.rem(me + j, count)
            pltpu.make_async_remote_copy(
                src_ref=buffer.at[phase, peer],
                dst_ref=buffer.at[phase, peer],
                send_sem=send_sem.at[phase, j],
                recv_sem=recv_sem.at[phase, peer],
                device_id=device(peer),
                device_id_type=MESH,
            ).wait_recv()
        for j in range(1, count):
            copy(j).wait_send()
        total = buffer[phase, 0]
        for j in range(1, count):
            total = total + buffer[phase, j]
        return total

    def all_reduce(phase, row):
        row = reduce_stage(phase, row, ar_depth, ard_send, ard_recv, depth, depth_count, lambda p: (sky, p))
        return reduce_stage(phase, row, ar_sky, ars_send, ars_recv, sky, sky_count, lambda p: (p, depth))

    send_all(0)

    for n in range(8):
        if near[n][3] is not None:

            def fill(n=n):
                for phase in range(4):
                    rcv[phase, n] = jnp.full(rcv.shape[2:], -FAR if phase == 0 else 0.0, jnp.float32)

            pl.when(jnp.logical_not(near[n][3]))(fill)

    def gather_left():
        for n in range(8):
            nid = near[n][2]
            for k in range(slots):
                cell = ipair_ref[0, nid, k]
                g = n * slots + k
                for i in range(3):
                    shift = ishift_ref[i, 0, nid, k].astype(jnp.float32)
                    lg[i, g : g + 1, :] = cl[i, pl.ds(cell, 1), :] - shift

    def rolled(refs, d, count):
        back = lax.rem(LANES - d, LANES)
        return [pltpu.roll(refs[i], back, 1) for i in range(3)]

    def rows_of(ref):
        return [ref[i] for i in range(3)]

    def self_counts():
        left = rows_of(cl)
        right = rows_of(cr)
        zero = tuple(jnp.zeros((8, LANES), jnp.float32) for _ in range(bins))
        ends = add_counts(zero, left, right)
        ends = add_counts(ends, left, [pltpu.roll(v, LANES // 2, 1) for v in right])
        sums = tuple(0.5 * v for v in ends)

        def body(d, sums):
            return add_counts(sums, left, rolled(right, d, cells))

        return lax.fori_loop(1, LANES // 2, body, sums)

    def ghost_counts(sums):
        def body(step, sums):
            left = rows_of(lg)
            right = rows_of(rg)
            for j in range(unroll):
                sums = add_counts(sums, left, rolled(right, step * unroll + j, ghosts))
            return sums

        return lax.fori_loop(0, LANES // unroll, body, sums)

    def slope(b):
        return coef[b : b + 1, :]

    def extra(b):
        return coef_x[b : b + 1, :]

    def ghost_forces():
        zero = tuple(jnp.zeros((ghosts, LANES), jnp.float32) for _ in range(6))

        def body(d, sums):
            left = rows_of(lg)
            right = rows_of(rg)
            force = pair_force(left, rolled(right, d, ghosts), slope, extra)
            to_left = tuple(sums[i] + force[i] for i in range(3))
            to_right = tuple(sums[3 + i] - pltpu.roll(force[i], d, 1) for i in range(3))
            return to_left + to_right

        return lax.fori_loop(0, LANES, body, zero)

    def self_forces():
        left = rows_of(cl)
        right = rows_of(cr)
        half = pair_force(left, [pltpu.roll(v, LANES // 2, 1) for v in right], slope, extra)

        def body(d, sums):
            force = pair_force(left, rolled(right, d, cells), slope, extra)
            return tuple(sums[i] + force[i] - pltpu.roll(force[i], d, 1) for i in range(3))

        return lax.fori_loop(1, LANES // 2, body, tuple(half))

    cell_rows = lax.broadcasted_iota(jnp.int32, (cells, LANES), 0)

    def scatter(total, row, cell):
        chosen = cell_rows == cell
        return [total[i] + jnp.where(chosen, row(i), 0.0) for i in range(3)]

    bin_rows = lax.broadcasted_iota(jnp.int32, (bins, LANES), 0)
    bin_lanes = lax.broadcasted_iota(jnp.int32, (bins, LANES), 1)
    on_diagonal = bin_rows == bin_lanes
    centre = bin_rows.astype(jnp.float32) + 0.5
    target = jnp.zeros((bins, LANES), jnp.float32)
    factor = jnp.zeros((bins, LANES), jnp.float32)
    for b in range(bins):
        target = jnp.where(bin_rows == b, target_ref[b], target)
    for anchor, members in GROUPS:
        for k in range(members):
            factor = jnp.where(bin_rows == anchor - k, bin_factor(anchor, k), factor)

    for step in range(STEPS):
        sums = self_counts()
        gather_left()
        if step == 0:
            receive_all(0)
            for n in range(8):
                for i in range(3):
                    rg[i, n * slots : (n + 1) * slots, :] = rcv[0, n, i * slots : (i + 1) * slots, :]
        else:
            receive_all(2)
            for n in range(8):
                for i in range(3):
                    moved = -rcv[2, n, i * slots : (i + 1) * slots, :] * inverse_rms
                    here = rg[i, n * slots : (n + 1) * slots, :]
                    rg[i, n * slots : (n + 1) * slots, :] = here + STEP_SIZE * moved
        sums = ghost_counts(sums)
        for b in range(bins):
            work[b : b + 1, :] = jnp.sum(sums[b], axis=0, keepdims=True)
        local = jnp.sum(work[...], axis=1, keepdims=True) * factor
        row = jnp.sum(jnp.where(on_diagonal, local, 0.0), axis=0, keepdims=True)
        row = all_reduce(2 * step, row)
        counts = jnp.sum(jnp.where(on_diagonal, row, 0.0), axis=1, keepdims=True)
        counts = jnp.broadcast_to(counts, (bins, LANES))
        mean_count = jnp.sum(counts, axis=0, keepdims=True) * (1.0 / bins)
        pull = (jnp.log(1.0 + counts) - target) * mean_count / (1.0 + counts)
        scaled_pull = pull * factor * -INV_WIDTH
        coef[...] = scaled_pull
        coef_x[...] = scaled_pull * centre

        forces = ghost_forces()
        back = 1 if step == 0 else 3
        for i in range(3):
            for n in range(8):
                snd[back, n, i * slots : (i + 1) * slots, :] = forces[3 + i][n * slots : (n + 1) * slots]
            row_grad[i] = forces[i]
        send_all(back)
        total = list(self_forces())
        for n in range(8):
            nid = near[n][2]
            for k in range(slots):
                g = n * slots + k
                total = scatter(total, lambda i: row_grad[i, g : g + 1, :], ipair_ref[0, nid, k])
        receive_all(back)
        for n in range(8):
            nid = near[n][2]
            for k in range(slots):
                total = scatter(
                    total, lambda i: rcv[back, n, i * slots + k : i * slots + k + 1, :], ecell_ref[0, nid, k]
                )
        if step + 1 < STEPS:
            for i in range(3):
                grad[i] = total[i]
            for n in range(8):
                nid = near[n][2]
                for k in range(slots):
                    cell = ecell_ref[0, nid, k]
                    for i in range(3):
                        snd[2, n, i * slots + k : i * slots + k + 1, :] = grad[i, pl.ds(cell, 1), :]
            send_all(2)
        power = total[0] * total[0] + total[1] * total[1] + total[2] * total[2]
        power = jnp.sum(jnp.sum(power, axis=0, keepdims=True), axis=1, keepdims=True)
        row = jnp.where(lane == 0, power, jnp.where(lane == 1, live_total, 0.0))
        row = all_reduce(2 * step + 1, row)
        power = jnp.sum(jnp.where(lane == 0, row, 0.0), axis=1, keepdims=True)
        live_all = jnp.sum(jnp.where(lane == 1, row, 0.0), axis=1, keepdims=True)
        inverse_rms = 1.0 / jnp.sqrt(power / (3.0 * live_all) + 1e-06)
        for i in range(3):
            move = -total[i] * inverse_rms
            if step == 0:
                out_ref[i] = move
            else:
                out_ref[i] = out_ref[i] + move
            if step + 1 < STEPS:
                cl[i] = cl[i] + STEP_SIZE * move
                cr[i] = cr[i] + STEP_SIZE * move

    for phase in range(4):
        drain_all(phase)


def body(sky_count, depth_count, positions, cell_points, target_log, export_count, export_cell, import_pair, import_shift):
    cells = positions.shape[1]
    slots = export_cell.shape[2]
    bins = target_log.shape[0]
    ghosts = 8 * slots
    vmem = pl.BlockSpec(memory_space=pltpu.VMEM)
    smem = pl.BlockSpec(memory_space=pltpu.SMEM)
    f32 = jnp.float32
    dma = pltpu.SemaphoreType.DMA
    return pl.pallas_call(
        functools.partial(kernel, sky_count, depth_count, slots, 2),
        out_shape=jax.ShapeDtypeStruct(positions.shape, f32),
        in_specs=[vmem] + [smem] * 6,
        out_specs=vmem,
        scratch_shapes=[
            pltpu.VMEM((3, cells, LANES), f32),
            pltpu.VMEM((3, cells, LANES), f32),
            pltpu.VMEM((3, ghosts, LANES), f32),
            pltpu.VMEM((3, ghosts, LANES), f32),
            pltpu.VMEM((3, cells, LANES), f32),
            pltpu.VMEM((bins, LANES), f32),
            pltpu.VMEM((bins, LANES), f32),
            pltpu.VMEM((bins, LANES), f32),
            pltpu.VMEM((3, ghosts, LANES), f32),
            pltpu.VMEM((4, 8, 3 * slots, LANES), f32),
            pltpu.VMEM((4, 8, 3 * slots, LANES), f32),
            pltpu.VMEM((4, depth_count, 1, LANES), f32),
            pltpu.VMEM((4, sky_count, 1, LANES), f32),
            dma((4, 8)),
            dma((4, 8)),
            dma((4, depth_count)),
            dma((4, depth_count)),
            dma((4, sky_count)),
            dma((4, sky_count)),
        ],
        compiler_params=pltpu.CompilerParams(collective_id=0, has_side_effects=True),
        name="descent",
    )(positions, cell_points, target_log, export_count, export_cell, import_pair, import_shift)


def solution(mesh):
    in_specs = (
        P(None, ("sky", "depth"), None),
        P(("sky", "depth")),
        P(),
        P(("sky", "depth"), None),
        P(("sky", "depth"), None, None),
        P(("sky", "depth"), None, None),
        P(None, ("sky", "depth"), None, None),
    )
    out_specs = P(None, ("sky", "depth"), None)
    run = functools.partial(body, mesh.shape["sky"], mesh.shape["depth"])
    return jax.shard_map(run, mesh=mesh, in_specs=in_specs, out_specs=out_specs, check_vma=False)
```

```python
import functools
import math

import jax
import jax.numpy as jnp
from jax import lax
from jax.experimental import pallas as pl
from jax.experimental.pallas import tpu as pltpu
from jax.sharding import PartitionSpec as P

STEPS = 2
EPS_SQ = 0.0001
INV_WIDTH = 16.0
STEP_SIZE = 0.01
GHOST_UNROLL = 4
SELF_UNROLL = 7
FAR = 10000.0
LANES = 128
MESH = pl.DeviceIdType.MESH

LOG2E = math.log2(math.e)
HALF_ROOT = math.sqrt(0.5 * LOG2E)
GROUPS = ((7, 8), (12, 5), (15, 3))
REGIONS = [(a, b) for a in (-1, 0, 1) for b in (-1, 0, 1) if (a, b) != (0, 0)]


def bin_factor(anchor, k):
    return math.exp(sum(anchor - j - 8 for j in range(k)))


def geometry(left, right):
    offs = [left[i] - right[i] for i in range(3)]
    square = offs[0] * offs[0] + offs[1] * offs[1] + (offs[2] * offs[2] + EPS_SQ)
    inverse = lax.rsqrt(square)
    scaled = (square * inverse) * (INV_WIDTH * HALF_ROOT)
    anchors = []
    for anchor, _ in GROUPS:
        gap = scaled - HALF_ROOT * (anchor + 0.5)
        anchors.append(jnp.exp2(-(gap * gap)))
    ratio = jnp.exp2(8.0 * LOG2E - scaled * (LOG2E / HALF_ROOT))
    return offs, inverse, scaled, anchors, ratio


def fold(value):
    total = value[0:8]
    for start in range(8, value.shape[0], 8):
        total = total + value[start : start + 8]
    return total


def add_counts(sums, left, right):
    _, _, _, anchors, ratio = geometry(left, right)
    sums = list(sums)
    for (anchor, members), term in zip(GROUPS, anchors):
        for k in range(members):
            if k:
                term = term * ratio
            sums[anchor - k] = sums[anchor - k] + fold(term)
    return tuple(sums)


def pair_force(left, right, slope, extra):
    offs, inverse, scaled, anchors, ratio = geometry(left, right)
    radius16 = scaled * (1.0 / HALF_ROOT)
    first = None
    second = None
    for (anchor, members), term in zip(GROUPS, anchors):
        poly = slope(anchor - members + 1)
        poly_extra = extra(anchor - members + 1)
        for k in range(members - 2, -1, -1):
            poly = poly * ratio + slope(anchor - k)
            poly_extra = poly_extra * ratio + extra(anchor - k)
        poly = poly * term
        poly_extra = poly_extra * term
        first = poly if first is None else first + poly
        second = poly_extra if second is None else second + poly_extra
    strength = (radius16 * first - second) * inverse
    return [strength * off for off in offs]


def kernel(
    sky_count, depth_count, slots,
    pos_ref, points_ref, target_ref, ecount_ref, ecell_ref, ipair_ref, ishift_ref,
    out_ref,
    cl, cr, lg, rg, grad, work, coef, coef_x, row_grad,
    snd, rcv, ar_depth, ar_sky,
    snd_sem, rcv_sem, ard_send, ard_recv, ars_send, ars_recv,
):
    bins = 16
    cells = pos_ref.shape[1]
    ghosts = 8 * slots
    sky = lax.axis_index("sky")
    depth = lax.axis_index("depth")

    near = []
    for across, along in REGIONS:
        there_sky = lax.rem(sky + across + sky_count, sky_count)
        there_depth = depth + along
        clamped = jnp.clip(there_depth, 0, depth_count - 1)
        if along == 0:
            valid = None
        elif along < 0:
            valid = depth > 0
        else:
            valid = depth < depth_count - 1
        near.append((there_sky, clamped, there_sky * depth_count + clamped, valid))

    def when_valid(valid, action):
        if valid is None:
            action()
        else:
            pl.when(valid)(action)

    barrier = pltpu.get_barrier_semaphore()

    def greet(there_sky, there_depth):
        pl.semaphore_signal(barrier, inc=1, device_id=(there_sky, there_depth), device_id_type=MESH)

    for j in range(1, sky_count):
        greet(lax.rem(sky + j, sky_count), depth)
    for j in range(1, depth_count):
        greet(sky, lax.rem(depth + j, depth_count))
    for (across, along), (there_sky, there_depth, _, valid) in zip(REGIONS, near):
        if across != 0 and along != 0:
            when_valid(valid, functools.partial(greet, there_sky, there_depth))

    lane = lax.broadcasted_iota(jnp.int32, (1, LANES), 1)
    live_total = jnp.zeros((1, LANES), jnp.float32)
    for c in range(cells):
        live = lane < points_ref[c]
        live_total = live_total + jnp.where(live, 1.0, 0.0)
        x = pos_ref[0, c : c + 1, :]
        cl[0, c : c + 1, :] = jnp.where(live, x, FAR)
        cr[0, c : c + 1, :] = jnp.where(live, x, -FAR)
    for i in (1, 2):
        cl[i] = pos_ref[i]
        cr[i] = pos_ref[i]
    live_total = jnp.sum(live_total, axis=1, keepdims=True)

    for n in range(8):
        nid = near[n][2]
        for k in range(slots):
            cell = ecell_ref[k, 0, nid]
            live = k < ecount_ref[0, nid]
            for i in range(3):
                row = cr[i, pl.ds(cell, 1), :]
                if i == 0:
                    row = jnp.where(live, row, -FAR)
                snd[0, n, i * slots + k : i * slots + k + 1, :] = row

    diagonals = 2 * jnp.where(depth > 0, 1, 0) + 2 * jnp.where(depth < depth_count - 1, 1, 0)
    pl.semaphore_wait(barrier, (sky_count - 1) + (depth_count - 1) + diagonals)

    def message(phase, n):
        there_sky, there_depth, _, _ = near[n]
        return pltpu.make_async_remote_copy(
            src_ref=snd.at[phase, n],
            dst_ref=rcv.at[phase, 7 - n],
            send_sem=snd_sem.at[phase, n],
            recv_sem=rcv_sem.at[phase, 7 - n],
            device_id=(there_sky, there_depth),
            device_id_type=MESH,
        )

    def arrival(phase, n):
        there_sky, there_depth, _, _ = near[n]
        return pltpu.make_async_remote_copy(
            src_ref=snd.at[phase, n],
            dst_ref=rcv.at[phase, n],
            send_sem=snd_sem.at[phase, n],
            recv_sem=rcv_sem.at[phase, n],
            device_id=(there_sky, there_depth),
            device_id_type=MESH,
        )

    def send_all(phase):
        for n in range(8):
            when_valid(near[n][3], lambda n=n: message(phase, n).start())

    def receive_all(phase):
        for n in range(8):
            when_valid(near[n][3], lambda n=n: arrival(phase, n).wait_recv())

    def drain_all(phase):
        for n in range(8):
            when_valid(near[n][3], lambda n=n: message(phase, n).wait_send())

    def reduce_stage(phase, row, buffer, send_sem, recv_sem, me, count, device):
        buffer[phase, me] = row

        def copy(j):
            peer = lax.rem(me + j, count)
            return pltpu.make_async_remote_copy(
                src_ref=buffer.at[phase, me],
                dst_ref=buffer.at[phase, me],
                send_sem=send_sem.at[phase, j],
                recv_sem=recv_sem.at[phase, me],
                device_id=device(peer),
                device_id_type=MESH,
            )

        for j in range(1, count):
            copy(j).start()
        for j in range(1, count):
            peer = lax.rem(me + j, count)
            pltpu.make_async_remote_copy(
                src_ref=buffer.at[phase, peer],
                dst_ref=buffer.at[phase, peer],
                send_sem=send_sem.at[phase, j],
                recv_sem=recv_sem.at[phase, peer],
                device_id=device(peer),
                device_id_type=MESH,
            ).wait_recv()
        for j in range(1, count):
            copy(j).wait_send()
        total = buffer[phase, 0]
        for j in range(1, count):
            total = total + buffer[phase, j]
        return total

    def all_reduce(phase, row):
        row = reduce_stage(phase, row, ar_depth, ard_send, ard_recv, depth, depth_count, lambda p: (sky, p))
        return reduce_stage(phase, row, ar_sky, ars_send, ars_recv, sky, sky_count, lambda p: (p, depth))

    send_all(0)

    for n in range(8):
        if near[n][3] is not None:

            def fill(n=n):
                for phase in range(4):
                    rcv[phase, n] = jnp.full(rcv.shape[2:], -FAR if phase == 0 else 0.0, jnp.float32)

            pl.when(jnp.logical_not(near[n][3]))(fill)

    def gather_left():
        for n in range(8):
            nid = near[n][2]
            for k in range(slots):
                cell = ipair_ref[k, 0, nid]
                g = n * slots + k
                for i in range(3):
                    shift = ishift_ref[i, k, 0, nid].astype(jnp.float32)
                    lg[i, g : g + 1, :] = cl[i, pl.ds(cell, 1), :] - shift

    def rolled(refs, d):
        back = lax.rem(LANES - d, LANES)
        return [pltpu.roll(refs[i], back, 1) for i in range(3)]

    def rows_of(ref):
        return [ref[i] for i in range(3)]

    def self_counts():
        left = rows_of(cl)
        right = rows_of(cr)
        zero = tuple(jnp.zeros((8, LANES), jnp.float32) for _ in range(bins))
        ends = add_counts(zero, left, right)
        ends = add_counts(ends, left, [pltpu.roll(v, LANES // 2, 1) for v in right])
        sums = tuple(0.5 * v for v in ends)

        def body(step, sums):
            for j in range(SELF_UNROLL):
                sums = add_counts(sums, left, rolled(right, 1 + step * SELF_UNROLL + j))
            return sums

        return lax.fori_loop(0, (LANES // 2 - 1) // SELF_UNROLL, body, sums)

    def ghost_counts(sums):
        def body(step, sums):
            left = rows_of(lg)
            right = rows_of(rg)
            for j in range(GHOST_UNROLL):
                sums = add_counts(sums, left, rolled(right, step * GHOST_UNROLL + j))
            return sums

        return lax.fori_loop(0, LANES // GHOST_UNROLL, body, sums)

    def slope(b):
        return coef[b : b + 1, :]

    def extra(b):
        return coef_x[b : b + 1, :]

    def ghost_forces():
        zero = tuple(jnp.zeros((ghosts, LANES), jnp.float32) for _ in range(6))

        def body(step, sums):
            left = rows_of(lg)
            right = rows_of(rg)
            for j in range(GHOST_UNROLL):
                d = step * GHOST_UNROLL + j
                force = pair_force(left, rolled(right, d), slope, extra)
                to_left = tuple(sums[i] + force[i] for i in range(3))
                to_right = tuple(sums[3 + i] - pltpu.roll(force[i], d, 1) for i in range(3))
                sums = to_left + to_right
            return sums

        return lax.fori_loop(0, LANES // GHOST_UNROLL, body, zero)

    def self_forces():
        left = rows_of(cl)
        right = rows_of(cr)
        half = pair_force(left, [pltpu.roll(v, LANES // 2, 1) for v in right], slope, extra)

        def body(step, sums):
            for j in range(SELF_UNROLL):
                d = 1 + step * SELF_UNROLL + j
                force = pair_force(left, rolled(right, d), slope, extra)
                sums = tuple(sums[i] + force[i] - pltpu.roll(force[i], d, 1) for i in range(3))
            return sums

        return lax.fori_loop(0, (LANES // 2 - 1) // SELF_UNROLL, body, tuple(half))

    cell_rows = lax.broadcasted_iota(jnp.int32, (cells, LANES), 0)

    def scatter(total, row, cell):
        chosen = cell_rows == cell
        return [total[i] + jnp.where(chosen, row(i), 0.0) for i in range(3)]

    bin_rows = lax.broadcasted_iota(jnp.int32, (bins, LANES), 0)
    bin_lanes = lax.broadcasted_iota(jnp.int32, (bins, LANES), 1)
    on_diagonal = bin_rows == bin_lanes
    centre = bin_rows.astype(jnp.float32) + 0.5
    target = jnp.zeros((bins, LANES), jnp.float32)
    factor = jnp.zeros((bins, LANES), jnp.float32)
    for b in range(bins):
        target = jnp.where(bin_rows == b, target_ref[b], target)
    for anchor, members in GROUPS:
        for k in range(members):
            factor = jnp.where(bin_rows == anchor - k, bin_factor(anchor, k), factor)

    for step in range(STEPS):
        sums = self_counts()
        gather_left()
        if step == 0:
            receive_all(0)
            for n in range(8):
                for i in range(3):
                    rg[i, n * slots : (n + 1) * slots, :] = rcv[0, n, i * slots : (i + 1) * slots, :]
        else:
            receive_all(2)
            for n in range(8):
                for i in range(3):
                    moved = -rcv[2, n, i * slots : (i + 1) * slots, :] * inverse_rms
                    here = rg[i, n * slots : (n + 1) * slots, :]
                    rg[i, n * slots : (n + 1) * slots, :] = here + STEP_SIZE * moved
        sums = ghost_counts(sums)
        for b in range(bins):
            work[b : b + 1, :] = jnp.sum(sums[b], axis=0, keepdims=True)
        local = jnp.sum(work[...], axis=1, keepdims=True) * factor
        row = jnp.sum(jnp.where(on_diagonal, local, 0.0), axis=0, keepdims=True)
        row = all_reduce(2 * step, row)
        counts = jnp.sum(jnp.where(on_diagonal, row, 0.0), axis=1, keepdims=True)
        counts = jnp.broadcast_to(counts, (bins, LANES))
        mean_count = jnp.sum(counts, axis=0, keepdims=True) * (1.0 / bins)
        pull = (jnp.log(1.0 + counts) - target) * mean_count / (1.0 + counts)
        scaled_pull = pull * factor * -INV_WIDTH
        coef[...] = scaled_pull
        coef_x[...] = scaled_pull * centre

        forces = ghost_forces()
        back = 1 if step == 0 else 3
        for i in range(3):
            for n in range(8):
                snd[back, n, i * slots : (i + 1) * slots, :] = forces[3 + i][n * slots : (n + 1) * slots]
            row_grad[i] = forces[i]
        send_all(back)
        total = list(self_forces())
        for n in range(8):
            nid = near[n][2]
            for k in range(slots):
                g = n * slots + k
                total = scatter(total, lambda i: row_grad[i, g : g + 1, :], ipair_ref[k, 0, nid])
        receive_all(back)
        for n in range(8):
            nid = near[n][2]
            for k in range(slots):
                total = scatter(
                    total, lambda i: rcv[back, n, i * slots + k : i * slots + k + 1, :], ecell_ref[k, 0, nid]
                )
        if step + 1 < STEPS:
            for i in range(3):
                grad[i] = total[i]
            for n in range(8):
                nid = near[n][2]
                for k in range(slots):
                    cell = ecell_ref[k, 0, nid]
                    for i in range(3):
                        snd[2, n, i * slots + k : i * slots + k + 1, :] = grad[i, pl.ds(cell, 1), :]
            send_all(2)
        power = total[0] * total[0] + total[1] * total[1] + total[2] * total[2]
        power = jnp.sum(jnp.sum(power, axis=0, keepdims=True), axis=1, keepdims=True)
        row = jnp.where(lane == 0, power, jnp.where(lane == 1, live_total, 0.0))
        row = all_reduce(2 * step + 1, row)
        power = jnp.sum(jnp.where(lane == 0, row, 0.0), axis=1, keepdims=True)
        live_all = jnp.sum(jnp.where(lane == 1, row, 0.0), axis=1, keepdims=True)
        inverse_rms = 1.0 / jnp.sqrt(power / (3.0 * live_all) + 1e-06)
        for i in range(3):
            move = -total[i] * inverse_rms
            if step == 0:
                out_ref[i] = move
            else:
                out_ref[i] = out_ref[i] + move
            if step + 1 < STEPS:
                cl[i] = cl[i] + STEP_SIZE * move
                cr[i] = cr[i] + STEP_SIZE * move

    for phase in range(4):
        drain_all(phase)


def body(sky_count, depth_count, positions, cell_points, target_log, export_count, export_cell, import_pair, import_shift):
    cells = positions.shape[1]
    slots = export_cell.shape[2]
    bins = target_log.shape[0]
    ghosts = 8 * slots
    vmem = pl.BlockSpec(memory_space=pltpu.VMEM)
    smem = pl.BlockSpec(memory_space=pltpu.SMEM)
    f32 = jnp.float32
    dma = pltpu.SemaphoreType.DMA
    return pl.pallas_call(
        functools.partial(kernel, sky_count, depth_count, slots),
        out_shape=jax.ShapeDtypeStruct(positions.shape, f32),
        in_specs=[vmem] + [smem] * 6,
        out_specs=vmem,
        scratch_shapes=[
            pltpu.VMEM((3, cells, LANES), f32),
            pltpu.VMEM((3, cells, LANES), f32),
            pltpu.VMEM((3, ghosts, LANES), f32),
            pltpu.VMEM((3, ghosts, LANES), f32),
            pltpu.VMEM((3, cells, LANES), f32),
            pltpu.VMEM((bins, LANES), f32),
            pltpu.VMEM((bins, LANES), f32),
            pltpu.VMEM((bins, LANES), f32),
            pltpu.VMEM((3, ghosts, LANES), f32),
            pltpu.VMEM((4, 8, 3 * slots, LANES), f32),
            pltpu.VMEM((4, 8, 3 * slots, LANES), f32),
            pltpu.VMEM((4, depth_count, 1, LANES), f32),
            pltpu.VMEM((4, sky_count, 1, LANES), f32),
            dma((4, 8)),
            dma((4, 8)),
            dma((4, depth_count)),
            dma((4, depth_count)),
            dma((4, sky_count)),
            dma((4, sky_count)),
        ],
        compiler_params=pltpu.CompilerParams(collective_id=0, has_side_effects=True),
        name="descent",
    )(
        positions,
        cell_points,
        target_log,
        export_count,
        jnp.transpose(export_cell, (2, 0, 1)),
        jnp.transpose(import_pair, (2, 0, 1)),
        jnp.transpose(import_shift, (0, 3, 1, 2)),
    )


def solution(mesh):
    in_specs = (
        P(None, ("sky", "depth"), None),
        P(("sky", "depth")),
        P(),
        P(("sky", "depth"), None),
        P(("sky", "depth"), None, None),
        P(("sky", "depth"), None, None),
        P(None, ("sky", "depth"), None, None),
    )
    out_specs = P(None, ("sky", "depth"), None)
    run = functools.partial(body, mesh.shape["sky"], mesh.shape["depth"])
    return jax.shard_map(run, mesh=mesh, in_specs=in_specs, out_specs=out_specs, check_vma=False)
```

```python
import functools
import math

import jax
import jax.numpy as jnp
from jax import lax
from jax.experimental import pallas as pl
from jax.experimental.pallas import tpu as pltpu
from jax.sharding import PartitionSpec as P

STEPS = 2
EPS_SQ = 0.0001
INV_WIDTH = 16.0
STEP_SIZE = 0.01
GHOST_UNROLL = 8
SELF_UNROLL = 9
FAR = 10000.0
LANES = 128
MESH = pl.DeviceIdType.MESH

LOG2E = math.log2(math.e)
HALF_ROOT = math.sqrt(0.5 * LOG2E)
GROUPS = ((7, 8), (12, 5), (15, 3))
REGIONS = [(a, b) for a in (-1, 0, 1) for b in (-1, 0, 1) if (a, b) != (0, 0)]


def bin_factor(anchor, k):
    return math.exp(sum(anchor - j - 8 for j in range(k)))


def geometry(left, right):
    offs = [left[i] - right[i] for i in range(3)]
    square = offs[0] * offs[0] + offs[1] * offs[1] + (offs[2] * offs[2] + EPS_SQ)
    inverse = lax.rsqrt(square)
    scaled = (square * inverse) * (INV_WIDTH * HALF_ROOT)
    anchors = []
    for anchor, _ in GROUPS:
        gap = scaled - HALF_ROOT * (anchor + 0.5)
        anchors.append(jnp.exp2(-(gap * gap)))
    ratio = jnp.exp2(8.0 * LOG2E - scaled * (LOG2E / HALF_ROOT))
    return offs, inverse, scaled, anchors, ratio


def fold(value):
    total = value[0:8]
    for start in range(8, value.shape[0], 8):
        total = total + value[start : start + 8]
    return total


def add_counts(sums, left, right):
    _, _, _, anchors, ratio = geometry(left, right)
    sums = list(sums)
    for (anchor, members), term in zip(GROUPS, anchors):
        for k in range(members):
            if k:
                term = term * ratio
            sums[anchor - k] = sums[anchor - k] + fold(term)
    return tuple(sums)


def pair_force(left, right, slope, extra):
    offs, inverse, scaled, anchors, ratio = geometry(left, right)
    radius16 = scaled * (1.0 / HALF_ROOT)
    first = None
    second = None
    for (anchor, members), term in zip(GROUPS, anchors):
        poly = slope(anchor - members + 1)
        poly_extra = extra(anchor - members + 1)
        for k in range(members - 2, -1, -1):
            poly = poly * ratio + slope(anchor - k)
            poly_extra = poly_extra * ratio + extra(anchor - k)
        poly = poly * term
        poly_extra = poly_extra * term
        first = poly if first is None else first + poly
        second = poly_extra if second is None else second + poly_extra
    strength = (radius16 * first - second) * inverse
    return [strength * off for off in offs]


def kernel(
    sky_count, depth_count, slots,
    pos_ref, points_ref, target_ref, ecount_ref, ecell_ref, ipair_ref, ishift_ref,
    out_ref,
    cl, cr, lg, rg, grad, work, coef, coef_x, row_grad,
    snd, rcv, ar_depth, ar_sky,
    snd_sem, rcv_sem, ard_send, ard_recv, ars_send, ars_recv,
):
    bins = 16
    cells = pos_ref.shape[1]
    ghosts = 8 * slots
    sky = lax.axis_index("sky")
    depth = lax.axis_index("depth")

    near = []
    for across, along in REGIONS:
        there_sky = lax.rem(sky + across + sky_count, sky_count)
        there_depth = depth + along
        clamped = jnp.clip(there_depth, 0, depth_count - 1)
        if along == 0:
            valid = None
        elif along < 0:
            valid = depth > 0
        else:
            valid = depth < depth_count - 1
        near.append((there_sky, clamped, there_sky * depth_count + clamped, valid))

    def when_valid(valid, action):
        if valid is None:
            action()
        else:
            pl.when(valid)(action)

    barrier = pltpu.get_barrier_semaphore()

    def greet(there_sky, there_depth):
        pl.semaphore_signal(barrier, inc=1, device_id=(there_sky, there_depth), device_id_type=MESH)

    for j in range(1, sky_count):
        greet(lax.rem(sky + j, sky_count), depth)
    for j in range(1, depth_count):
        greet(sky, lax.rem(depth + j, depth_count))
    for (across, along), (there_sky, there_depth, _, valid) in zip(REGIONS, near):
        if across != 0 and along != 0:
            when_valid(valid, functools.partial(greet, there_sky, there_depth))

    lane = lax.broadcasted_iota(jnp.int32, (1, LANES), 1)
    live_total = jnp.zeros((1, LANES), jnp.float32)
    for c in range(cells):
        live = lane < points_ref[c]
        live_total = live_total + jnp.where(live, 1.0, 0.0)
        x = pos_ref[0, c : c + 1, :]
        cl[0, c : c + 1, :] = jnp.where(live, x, FAR)
        cr[0, c : c + 1, :] = jnp.where(live, x, -FAR)
    for i in (1, 2):
        cl[i] = pos_ref[i]
        cr[i] = pos_ref[i]
    live_total = jnp.sum(live_total, axis=1, keepdims=True)

    for n in range(8):
        nid = near[n][2]
        for k in range(slots):
            cell = ecell_ref[k, 0, nid]
            live = k < ecount_ref[0, nid]
            for i in range(3):
                row = cr[i, pl.ds(cell, 1), :]
                if i == 0:
                    row = jnp.where(live, row, -FAR)
                snd[0, n, i * slots + k : i * slots + k + 1, :] = row

    diagonals = 2 * jnp.where(depth > 0, 1, 0) + 2 * jnp.where(depth < depth_count - 1, 1, 0)
    pl.semaphore_wait(barrier, (sky_count - 1) + (depth_count - 1) + diagonals)

    def message(phase, n):
        there_sky, there_depth, _, _ = near[n]
        return pltpu.make_async_remote_copy(
            src_ref=snd.at[phase, n],
            dst_ref=rcv.at[phase, 7 - n],
            send_sem=snd_sem.at[phase, n],
            recv_sem=rcv_sem.at[phase, 7 - n],
            device_id=(there_sky, there_depth),
            device_id_type=MESH,
        )

    def arrival(phase, n):
        there_sky, there_depth, _, _ = near[n]
        return pltpu.make_async_remote_copy(
            src_ref=snd.at[phase, n],
            dst_ref=rcv.at[phase, n],
            send_sem=snd_sem.at[phase, n],
            recv_sem=rcv_sem.at[phase, n],
            device_id=(there_sky, there_depth),
            device_id_type=MESH,
        )

    def send_all(phase):
        for n in range(8):
            when_valid(near[n][3], lambda n=n: message(phase, n).start())

    def receive_all(phase):
        for n in range(8):
            when_valid(near[n][3], lambda n=n: arrival(phase, n).wait_recv())

    def drain_all(phase):
        for n in range(8):
            when_valid(near[n][3], lambda n=n: message(phase, n).wait_send())

    def reduce_stage(phase, row, buffer, send_sem, recv_sem, me, count, device):
        buffer[phase, me] = row

        def copy(j):
            peer = lax.rem(me + j, count)
            return pltpu.make_async_remote_copy(
                src_ref=buffer.at[phase, me],
                dst_ref=buffer.at[phase, me],
                send_sem=send_sem.at[phase, j],
                recv_sem=recv_sem.at[phase, me],
                device_id=device(peer),
                device_id_type=MESH,
            )

        for j in range(1, count):
            copy(j).start()
        for j in range(1, count):
            peer = lax.rem(me + j, count)
            pltpu.make_async_remote_copy(
                src_ref=buffer.at[phase, peer],
                dst_ref=buffer.at[phase, peer],
                send_sem=send_sem.at[phase, j],
                recv_sem=recv_sem.at[phase, peer],
                device_id=device(peer),
                device_id_type=MESH,
            ).wait_recv()
        for j in range(1, count):
            copy(j).wait_send()
        total = buffer[phase, 0]
        for j in range(1, count):
            total = total + buffer[phase, j]
        return total

    def all_reduce(phase, row):
        row = reduce_stage(phase, row, ar_depth, ard_send, ard_recv, depth, depth_count, lambda p: (sky, p))
        return reduce_stage(phase, row, ar_sky, ars_send, ars_recv, sky, sky_count, lambda p: (p, depth))

    send_all(0)

    for n in range(8):
        if near[n][3] is not None:

            def fill(n=n):
                for phase in range(4):
                    rcv[phase, n] = jnp.full(rcv.shape[2:], -FAR if phase == 0 else 0.0, jnp.float32)

            pl.when(jnp.logical_not(near[n][3]))(fill)

    def gather_left():
        for n in range(8):
            nid = near[n][2]
            for k in range(slots):
                cell = ipair_ref[k, 0, nid]
                g = n * slots + k
                for i in range(3):
                    shift = ishift_ref[i, k, 0, nid].astype(jnp.float32)
                    lg[i, g : g + 1, :] = cl[i, pl.ds(cell, 1), :] - shift

    def rolled(refs, d):
        back = lax.rem(LANES - d, LANES)
        return [pltpu.roll(refs[i], back, 1) for i in range(3)]

    def rows_of(ref):
        return [ref[i] for i in range(3)]

    def self_counts():
        left = rows_of(cl)
        right = rows_of(cr)
        zero = tuple(jnp.zeros((8, LANES), jnp.float32) for _ in range(bins))
        ends = add_counts(zero, left, right)
        ends = add_counts(ends, left, [pltpu.roll(v, LANES // 2, 1) for v in right])
        sums = tuple(0.5 * v for v in ends)

        def body(step, sums):
            for j in range(SELF_UNROLL):
                sums = add_counts(sums, left, rolled(right, 1 + step * SELF_UNROLL + j))
            return sums

        return lax.fori_loop(0, (LANES // 2 - 1) // SELF_UNROLL, body, sums)

    def ghost_counts(sums):
        def body(step, sums):
            left = rows_of(lg)
            right = rows_of(rg)
            for j in range(GHOST_UNROLL):
                sums = add_counts(sums, left, rolled(right, step * GHOST_UNROLL + j))
            return sums

        return lax.fori_loop(0, LANES // GHOST_UNROLL, body, sums)

    def slope(b):
        return coef[b : b + 1, :]

    def extra(b):
        return coef_x[b : b + 1, :]

    def ghost_forces():
        zero = tuple(jnp.zeros((ghosts, LANES), jnp.float32) for _ in range(6))

        def body(step, sums):
            left = rows_of(lg)
            right = rows_of(rg)
            for j in range(GHOST_UNROLL):
                d = step * GHOST_UNROLL + j
                force = pair_force(left, rolled(right, d), slope, extra)
                to_left = tuple(sums[i] + force[i] for i in range(3))
                to_right = tuple(sums[3 + i] - pltpu.roll(force[i], d, 1) for i in range(3))
                sums = to_left + to_right
            return sums

        return lax.fori_loop(0, LANES // GHOST_UNROLL, body, zero)

    def self_forces():
        left = rows_of(cl)
        right = rows_of(cr)
        half = pair_force(left, [pltpu.roll(v, LANES // 2, 1) for v in right], slope, extra)

        def body(step, sums):
            for j in range(SELF_UNROLL):
                d = 1 + step * SELF_UNROLL + j
                force = pair_force(left, rolled(right, d), slope, extra)
                sums = tuple(sums[i] + force[i] - pltpu.roll(force[i], d, 1) for i in range(3))
            return sums

        return lax.fori_loop(0, (LANES // 2 - 1) // SELF_UNROLL, body, tuple(half))

    cell_rows = lax.broadcasted_iota(jnp.int32, (cells, LANES), 0)

    def scatter(total, row, cell):
        chosen = cell_rows == cell
        return [total[i] + jnp.where(chosen, row(i), 0.0) for i in range(3)]

    bin_rows = lax.broadcasted_iota(jnp.int32, (bins, LANES), 0)
    bin_lanes = lax.broadcasted_iota(jnp.int32, (bins, LANES), 1)
    on_diagonal = bin_rows == bin_lanes
    centre = bin_rows.astype(jnp.float32) + 0.5
    target = jnp.zeros((bins, LANES), jnp.float32)
    factor = jnp.zeros((bins, LANES), jnp.float32)
    for b in range(bins):
        target = jnp.where(bin_rows == b, target_ref[b], target)
    for anchor, members in GROUPS:
        for k in range(members):
            factor = jnp.where(bin_rows == anchor - k, bin_factor(anchor, k), factor)

    for step in range(STEPS):
        sums = self_counts()
        gather_left()
        if step == 0:
            receive_all(0)
            for n in range(8):
                for i in range(3):
                    rg[i, n * slots : (n + 1) * slots, :] = rcv[0, n, i * slots : (i + 1) * slots, :]
        else:
            receive_all(2)
            for n in range(8):
                for i in range(3):
                    moved = -rcv[2, n, i * slots : (i + 1) * slots, :] * inverse_rms
                    here = rg[i, n * slots : (n + 1) * slots, :]
                    rg[i, n * slots : (n + 1) * slots, :] = here + STEP_SIZE * moved
        sums = ghost_counts(sums)
        for b in range(bins):
            work[b : b + 1, :] = jnp.sum(sums[b], axis=0, keepdims=True)
        local = jnp.sum(work[...], axis=1, keepdims=True) * factor
        row = jnp.sum(jnp.where(on_diagonal, local, 0.0), axis=0, keepdims=True)
        row = all_reduce(2 * step, row)
        counts = jnp.sum(jnp.where(on_diagonal, row, 0.0), axis=1, keepdims=True)
        counts = jnp.broadcast_to(counts, (bins, LANES))
        mean_count = jnp.sum(counts, axis=0, keepdims=True) * (1.0 / bins)
        pull = (jnp.log(1.0 + counts) - target) * mean_count / (1.0 + counts)
        scaled_pull = pull * factor * -INV_WIDTH
        coef[...] = scaled_pull
        coef_x[...] = scaled_pull * centre

        forces = ghost_forces()
        back = 1 if step == 0 else 3
        for i in range(3):
            for n in range(8):
                snd[back, n, i * slots : (i + 1) * slots, :] = forces[3 + i][n * slots : (n + 1) * slots]
            row_grad[i] = forces[i]
        send_all(back)
        total = list(self_forces())
        for n in range(8):
            nid = near[n][2]
            for k in range(slots):
                g = n * slots + k
                total = scatter(total, lambda i: row_grad[i, g : g + 1, :], ipair_ref[k, 0, nid])
        receive_all(back)
        for n in range(8):
            nid = near[n][2]
            for k in range(slots):
                total = scatter(
                    total, lambda i: rcv[back, n, i * slots + k : i * slots + k + 1, :], ecell_ref[k, 0, nid]
                )
        if step + 1 < STEPS:
            for i in range(3):
                grad[i] = total[i]
            for n in range(8):
                nid = near[n][2]
                for k in range(slots):
                    cell = ecell_ref[k, 0, nid]
                    for i in range(3):
                        snd[2, n, i * slots + k : i * slots + k + 1, :] = grad[i, pl.ds(cell, 1), :]
            send_all(2)
        power = total[0] * total[0] + total[1] * total[1] + total[2] * total[2]
        power = jnp.sum(jnp.sum(power, axis=0, keepdims=True), axis=1, keepdims=True)
        row = jnp.where(lane == 0, power, jnp.where(lane == 1, live_total, 0.0))
        row = all_reduce(2 * step + 1, row)
        power = jnp.sum(jnp.where(lane == 0, row, 0.0), axis=1, keepdims=True)
        live_all = jnp.sum(jnp.where(lane == 1, row, 0.0), axis=1, keepdims=True)
        inverse_rms = 1.0 / jnp.sqrt(power / (3.0 * live_all) + 1e-06)
        for i in range(3):
            move = -total[i] * inverse_rms
            if step == 0:
                out_ref[i] = move
            else:
                out_ref[i] = out_ref[i] + move
            if step + 1 < STEPS:
                cl[i] = cl[i] + STEP_SIZE * move
                cr[i] = cr[i] + STEP_SIZE * move

    for phase in range(4):
        drain_all(phase)


def body(sky_count, depth_count, positions, cell_points, target_log, export_count, export_cell, import_pair, import_shift):
    cells = positions.shape[1]
    slots = export_cell.shape[2]
    bins = target_log.shape[0]
    ghosts = 8 * slots
    vmem = pl.BlockSpec(memory_space=pltpu.VMEM)
    smem = pl.BlockSpec(memory_space=pltpu.SMEM)
    f32 = jnp.float32
    dma = pltpu.SemaphoreType.DMA
    return pl.pallas_call(
        functools.partial(kernel, sky_count, depth_count, slots),
        out_shape=jax.ShapeDtypeStruct(positions.shape, f32),
        in_specs=[vmem] + [smem] * 6,
        out_specs=vmem,
        scratch_shapes=[
            pltpu.VMEM((3, cells, LANES), f32),
            pltpu.VMEM((3, cells, LANES), f32),
            pltpu.VMEM((3, ghosts, LANES), f32),
            pltpu.VMEM((3, ghosts, LANES), f32),
            pltpu.VMEM((3, cells, LANES), f32),
            pltpu.VMEM((bins, LANES), f32),
            pltpu.VMEM((bins, LANES), f32),
            pltpu.VMEM((bins, LANES), f32),
            pltpu.VMEM((3, ghosts, LANES), f32),
            pltpu.VMEM((4, 8, 3 * slots, LANES), f32),
            pltpu.VMEM((4, 8, 3 * slots, LANES), f32),
            pltpu.VMEM((4, depth_count, 1, LANES), f32),
            pltpu.VMEM((4, sky_count, 1, LANES), f32),
            dma((4, 8)),
            dma((4, 8)),
            dma((4, depth_count)),
            dma((4, depth_count)),
            dma((4, sky_count)),
            dma((4, sky_count)),
        ],
        compiler_params=pltpu.CompilerParams(collective_id=0, has_side_effects=True),
        name="descent",
    )(
        positions,
        cell_points,
        target_log,
        export_count,
        jnp.transpose(export_cell, (2, 0, 1)),
        jnp.transpose(import_pair, (2, 0, 1)),
        jnp.transpose(import_shift, (0, 3, 1, 2)),
    )


def solution(mesh):
    in_specs = (
        P(None, ("sky", "depth"), None),
        P(("sky", "depth")),
        P(),
        P(("sky", "depth"), None),
        P(("sky", "depth"), None, None),
        P(("sky", "depth"), None, None),
        P(None, ("sky", "depth"), None, None),
    )
    out_specs = P(None, ("sky", "depth"), None)
    run = functools.partial(body, mesh.shape["sky"], mesh.shape["depth"])
    return jax.shard_map(run, mesh=mesh, in_specs=in_specs, out_specs=out_specs, check_vma=False)
```

```python
import functools
import math

import jax
import jax.numpy as jnp
from jax import lax
from jax.experimental import pallas as pl
from jax.experimental.pallas import tpu as pltpu
from jax.sharding import PartitionSpec as P

STEPS = 2
EPS_SQ = 0.0001
INV_WIDTH = 16.0
STEP_SIZE = 0.01
GHOST_UNROLL = 8
SELF_UNROLL = 9
FIELDS = 9
FAR = 10000.0
LANES = 128
MESH = pl.DeviceIdType.MESH

LOG2E = math.log2(math.e)
HALF_ROOT = math.sqrt(0.5 * LOG2E)
GROUPS = ((7, 8), (12, 5), (15, 3))
REGIONS = [(a, b) for a in (-1, 0, 1) for b in (-1, 0, 1) if (a, b) != (0, 0)]


def bin_factor(anchor, k):
    return math.exp(sum(anchor - j - 8 for j in range(k)))


def geometry(left, right):
    offs = [left[i] - right[i] for i in range(3)]
    square = offs[0] * offs[0] + offs[1] * offs[1] + (offs[2] * offs[2] + EPS_SQ)
    inverse = lax.rsqrt(square)
    scaled = (square * inverse) * (INV_WIDTH * HALF_ROOT)
    anchors = []
    for anchor, _ in GROUPS:
        gap = scaled - HALF_ROOT * (anchor + 0.5)
        anchors.append(jnp.exp2(-(gap * gap)))
    ratio = jnp.exp2(8.0 * LOG2E - scaled * (LOG2E / HALF_ROOT))
    return offs + [inverse, scaled, ratio] + anchors


def fold(value):
    total = value[0:8]
    for start in range(8, value.shape[0], 8):
        total = total + value[start : start + 8]
    return total


def add_counts(sums, fields):
    ratio = fields[5]
    anchors = fields[6:]
    sums = list(sums)
    for (anchor, members), term in zip(GROUPS, anchors):
        for k in range(members):
            if k:
                term = term * ratio
            sums[anchor - k] = sums[anchor - k] + fold(term)
    return tuple(sums)


def pair_force(fields, slope, extra):
    offs = fields[:3]
    inverse, scaled, ratio = fields[3:6]
    anchors = fields[6:]
    first = None
    second = None
    for (anchor, members), term in zip(GROUPS, anchors):
        poly = slope(anchor - members + 1)
        poly_extra = extra(anchor - members + 1)
        for k in range(members - 2, -1, -1):
            poly = poly * ratio + slope(anchor - k)
            poly_extra = poly_extra * ratio + extra(anchor - k)
        poly = poly * term
        poly_extra = poly_extra * term
        first = poly if first is None else first + poly
        second = poly_extra if second is None else second + poly_extra
    strength = (scaled * first - second) * inverse
    return [strength * off for off in offs]


def kernel(
    sky_count, depth_count, slots,
    pos_ref, points_ref, target_ref, ecount_ref, ecell_ref, ipair_ref, ishift_ref,
    out_ref,
    cl, cr, lg, rg, grad, work, coef, coef_x, row_grad,
    snd, rcv, ar_depth, ar_sky, self_fields, ghost_fields,
    snd_sem, rcv_sem, ard_send, ard_recv, ars_send, ars_recv,
):
    bins = 16
    cells = pos_ref.shape[1]
    ghosts = 8 * slots
    sky = lax.axis_index("sky")
    depth = lax.axis_index("depth")

    near = []
    for across, along in REGIONS:
        there_sky = lax.rem(sky + across + sky_count, sky_count)
        there_depth = depth + along
        clamped = jnp.clip(there_depth, 0, depth_count - 1)
        if along == 0:
            valid = None
        elif along < 0:
            valid = depth > 0
        else:
            valid = depth < depth_count - 1
        near.append((there_sky, clamped, there_sky * depth_count + clamped, valid))

    def when_valid(valid, action):
        if valid is None:
            action()
        else:
            pl.when(valid)(action)

    barrier = pltpu.get_barrier_semaphore()

    def greet(there_sky, there_depth):
        pl.semaphore_signal(barrier, inc=1, device_id=(there_sky, there_depth), device_id_type=MESH)

    for j in range(1, sky_count):
        greet(lax.rem(sky + j, sky_count), depth)
    for j in range(1, depth_count):
        greet(sky, lax.rem(depth + j, depth_count))
    for (across, along), (there_sky, there_depth, _, valid) in zip(REGIONS, near):
        if across != 0 and along != 0:
            when_valid(valid, functools.partial(greet, there_sky, there_depth))

    lane = lax.broadcasted_iota(jnp.int32, (1, LANES), 1)
    live_total = jnp.zeros((1, LANES), jnp.float32)
    for c in range(cells):
        live = lane < points_ref[c]
        live_total = live_total + jnp.where(live, 1.0, 0.0)
        x = pos_ref[0, c : c + 1, :]
        cl[0, c : c + 1, :] = jnp.where(live, x, FAR)
        cr[0, c : c + 1, :] = jnp.where(live, x, -FAR)
    for i in (1, 2):
        cl[i] = pos_ref[i]
        cr[i] = pos_ref[i]
    live_total = jnp.sum(live_total, axis=1, keepdims=True)

    for n in range(8):
        nid = near[n][2]
        for k in range(slots):
            cell = ecell_ref[k, 0, nid]
            live = k < ecount_ref[0, nid]
            for i in range(3):
                row = cr[i, pl.ds(cell, 1), :]
                if i == 0:
                    row = jnp.where(live, row, -FAR)
                snd[0, n, i * slots + k : i * slots + k + 1, :] = row

    diagonals = 2 * jnp.where(depth > 0, 1, 0) + 2 * jnp.where(depth < depth_count - 1, 1, 0)
    pl.semaphore_wait(barrier, (sky_count - 1) + (depth_count - 1) + diagonals)

    def message(phase, n):
        there_sky, there_depth, _, _ = near[n]
        return pltpu.make_async_remote_copy(
            src_ref=snd.at[phase, n],
            dst_ref=rcv.at[phase, 7 - n],
            send_sem=snd_sem.at[phase, n],
            recv_sem=rcv_sem.at[phase, 7 - n],
            device_id=(there_sky, there_depth),
            device_id_type=MESH,
        )

    def arrival(phase, n):
        there_sky, there_depth, _, _ = near[n]
        return pltpu.make_async_remote_copy(
            src_ref=snd.at[phase, n],
            dst_ref=rcv.at[phase, n],
            send_sem=snd_sem.at[phase, n],
            recv_sem=rcv_sem.at[phase, n],
            device_id=(there_sky, there_depth),
            device_id_type=MESH,
        )

    def send_all(phase):
        for n in range(8):
            when_valid(near[n][3], lambda n=n: message(phase, n).start())

    def receive_all(phase):
        for n in range(8):
            when_valid(near[n][3], lambda n=n: arrival(phase, n).wait_recv())

    def drain_all(phase):
        for n in range(8):
            when_valid(near[n][3], lambda n=n: message(phase, n).wait_send())

    def reduce_stage(phase, row, buffer, send_sem, recv_sem, me, count, device):
        buffer[phase, me] = row

        def copy(j):
            peer = lax.rem(me + j, count)
            return pltpu.make_async_remote_copy(
                src_ref=buffer.at[phase, me],
                dst_ref=buffer.at[phase, me],
                send_sem=send_sem.at[phase, j],
                recv_sem=recv_sem.at[phase, me],
                device_id=device(peer),
                device_id_type=MESH,
            )

        for j in range(1, count):
            copy(j).start()
        for j in range(1, count):
            peer = lax.rem(me + j, count)
            pltpu.make_async_remote_copy(
                src_ref=buffer.at[phase, peer],
                dst_ref=buffer.at[phase, peer],
                send_sem=send_sem.at[phase, j],
                recv_sem=recv_sem.at[phase, peer],
                device_id=device(peer),
                device_id_type=MESH,
            ).wait_recv()
        for j in range(1, count):
            copy(j).wait_send()
        total = buffer[phase, 0]
        for j in range(1, count):
            total = total + buffer[phase, j]
        return total

    def all_reduce(phase, row):
        row = reduce_stage(phase, row, ar_depth, ard_send, ard_recv, depth, depth_count, lambda p: (sky, p))
        return reduce_stage(phase, row, ar_sky, ars_send, ars_recv, sky, sky_count, lambda p: (p, depth))

    send_all(0)

    for n in range(8):
        if near[n][3] is not None:

            def fill(n=n):
                for phase in range(4):
                    rcv[phase, n] = jnp.full(rcv.shape[2:], -FAR if phase == 0 else 0.0, jnp.float32)

            pl.when(jnp.logical_not(near[n][3]))(fill)

    def gather_left():
        for n in range(8):
            nid = near[n][2]
            for k in range(slots):
                cell = ipair_ref[k, 0, nid]
                g = n * slots + k
                for i in range(3):
                    shift = ishift_ref[i, k, 0, nid].astype(jnp.float32)
                    lg[i, g : g + 1, :] = cl[i, pl.ds(cell, 1), :] - shift

    def rolled(refs, d):
        back = lax.rem(LANES - d, LANES)
        return [pltpu.roll(refs[i], back, 1) for i in range(3)]

    def rows_of(ref):
        return [ref[i] for i in range(3)]

    def save(ref, at, fields):
        for f, value in enumerate(fields):
            ref[at, f] = value

    def kept(ref, at):
        return [ref[at, f] for f in range(FIELDS)]

    def self_counts():
        left = rows_of(cl)
        right = rows_of(cr)
        zero = tuple(jnp.zeros((8, LANES), jnp.float32) for _ in range(bins))
        ends = add_counts(zero, geometry(left, right))
        ends = add_counts(ends, geometry(left, [pltpu.roll(v, LANES // 2, 1) for v in right]))
        sums = tuple(0.5 * v for v in ends)

        def body(step, sums):
            for j in range(SELF_UNROLL):
                fields = geometry(left, rolled(right, 1 + step * SELF_UNROLL + j))
                save(self_fields, step * SELF_UNROLL + j, fields)
                sums = add_counts(sums, fields)
            return sums

        return lax.fori_loop(0, (LANES // 2 - 1) // SELF_UNROLL, body, sums)

    def ghost_counts(sums):
        def body(step, sums):
            left = rows_of(lg)
            right = rows_of(rg)
            for j in range(GHOST_UNROLL):
                d = step * GHOST_UNROLL + j
                fields = geometry(left, rolled(right, d))
                save(ghost_fields, d, fields)
                sums = add_counts(sums, fields)
            return sums

        return lax.fori_loop(0, LANES // GHOST_UNROLL, body, sums)

    def slope(b):
        return coef[b : b + 1, :]

    def extra(b):
        return coef_x[b : b + 1, :]

    def ghost_forces():
        zero = tuple(jnp.zeros((ghosts, LANES), jnp.float32) for _ in range(6))

        def body(step, sums):
            for j in range(GHOST_UNROLL):
                d = step * GHOST_UNROLL + j
                force = pair_force(kept(ghost_fields, d), slope, extra)
                to_left = tuple(sums[i] + force[i] for i in range(3))
                to_right = tuple(sums[3 + i] - pltpu.roll(force[i], d, 1) for i in range(3))
                sums = to_left + to_right
            return sums

        return lax.fori_loop(0, LANES // GHOST_UNROLL, body, zero)

    def self_forces():
        left = rows_of(cl)
        right = rows_of(cr)
        half = pair_force(geometry(left, [pltpu.roll(v, LANES // 2, 1) for v in right]), slope, extra)

        def body(step, sums):
            for j in range(SELF_UNROLL):
                d = 1 + step * SELF_UNROLL + j
                force = pair_force(kept(self_fields, d - 1), slope, extra)
                sums = tuple(sums[i] + force[i] - pltpu.roll(force[i], d, 1) for i in range(3))
            return sums

        return lax.fori_loop(0, (LANES // 2 - 1) // SELF_UNROLL, body, tuple(half))

    cell_rows = lax.broadcasted_iota(jnp.int32, (cells, LANES), 0)

    def scatter(total, row, cell):
        chosen = cell_rows == cell
        return [total[i] + jnp.where(chosen, row(i), 0.0) for i in range(3)]

    bin_rows = lax.broadcasted_iota(jnp.int32, (bins, LANES), 0)
    bin_lanes = lax.broadcasted_iota(jnp.int32, (bins, LANES), 1)
    on_diagonal = bin_rows == bin_lanes
    centre = bin_rows.astype(jnp.float32) + 0.5
    target = jnp.zeros((bins, LANES), jnp.float32)
    factor = jnp.zeros((bins, LANES), jnp.float32)
    for b in range(bins):
        target = jnp.where(bin_rows == b, target_ref[b], target)
    for anchor, members in GROUPS:
        for k in range(members):
            factor = jnp.where(bin_rows == anchor - k, bin_factor(anchor, k), factor)

    for step in range(STEPS):
        sums = self_counts()
        gather_left()
        if step == 0:
            receive_all(0)
            for n in range(8):
                for i in range(3):
                    rg[i, n * slots : (n + 1) * slots, :] = rcv[0, n, i * slots : (i + 1) * slots, :]
        else:
            receive_all(2)
            for n in range(8):
                for i in range(3):
                    moved = -rcv[2, n, i * slots : (i + 1) * slots, :] * inverse_rms
                    here = rg[i, n * slots : (n + 1) * slots, :]
                    rg[i, n * slots : (n + 1) * slots, :] = here + STEP_SIZE * moved
        sums = ghost_counts(sums)
        for b in range(bins):
            work[b : b + 1, :] = jnp.sum(sums[b], axis=0, keepdims=True)
        local = jnp.sum(work[...], axis=1, keepdims=True) * factor
        row = jnp.sum(jnp.where(on_diagonal, local, 0.0), axis=0, keepdims=True)
        row = all_reduce(2 * step, row)
        counts = jnp.sum(jnp.where(on_diagonal, row, 0.0), axis=1, keepdims=True)
        counts = jnp.broadcast_to(counts, (bins, LANES))
        mean_count = jnp.sum(counts, axis=0, keepdims=True) * (1.0 / bins)
        pull = (jnp.log(1.0 + counts) - target) * mean_count / (1.0 + counts)
        scaled_pull = pull * factor * -INV_WIDTH
        coef[...] = scaled_pull * (1.0 / HALF_ROOT)
        coef_x[...] = scaled_pull * centre

        forces = ghost_forces()
        back = 1 if step == 0 else 3
        for i in range(3):
            for n in range(8):
                snd[back, n, i * slots : (i + 1) * slots, :] = forces[3 + i][n * slots : (n + 1) * slots]
            row_grad[i] = forces[i]
        send_all(back)
        total = list(self_forces())
        for n in range(8):
            nid = near[n][2]
            for k in range(slots):
                g = n * slots + k
                total = scatter(total, lambda i: row_grad[i, g : g + 1, :], ipair_ref[k, 0, nid])
        receive_all(back)
        for n in range(8):
            nid = near[n][2]
            for k in range(slots):
                total = scatter(
                    total, lambda i: rcv[back, n, i * slots + k : i * slots + k + 1, :], ecell_ref[k, 0, nid]
                )
        if step + 1 < STEPS:
            for i in range(3):
                grad[i] = total[i]
            for n in range(8):
                nid = near[n][2]
                for k in range(slots):
                    cell = ecell_ref[k, 0, nid]
                    for i in range(3):
                        snd[2, n, i * slots + k : i * slots + k + 1, :] = grad[i, pl.ds(cell, 1), :]
            send_all(2)
        power = total[0] * total[0] + total[1] * total[1] + total[2] * total[2]
        power = jnp.sum(jnp.sum(power, axis=0, keepdims=True), axis=1, keepdims=True)
        row = jnp.where(lane == 0, power, jnp.where(lane == 1, live_total, 0.0))
        row = all_reduce(2 * step + 1, row)
        power = jnp.sum(jnp.where(lane == 0, row, 0.0), axis=1, keepdims=True)
        live_all = jnp.sum(jnp.where(lane == 1, row, 0.0), axis=1, keepdims=True)
        inverse_rms = 1.0 / jnp.sqrt(power / (3.0 * live_all) + 1e-06)
        for i in range(3):
            move = -total[i] * inverse_rms
            if step == 0:
                out_ref[i] = move
            else:
                out_ref[i] = out_ref[i] + move
            if step + 1 < STEPS:
                cl[i] = cl[i] + STEP_SIZE * move
                cr[i] = cr[i] + STEP_SIZE * move

    for phase in range(4):
        drain_all(phase)


def body(sky_count, depth_count, positions, cell_points, target_log, export_count, export_cell, import_pair, import_shift):
    cells = positions.shape[1]
    slots = export_cell.shape[2]
    bins = target_log.shape[0]
    ghosts = 8 * slots
    vmem = pl.BlockSpec(memory_space=pltpu.VMEM)
    smem = pl.BlockSpec(memory_space=pltpu.SMEM)
    f32 = jnp.float32
    dma = pltpu.SemaphoreType.DMA
    return pl.pallas_call(
        functools.partial(kernel, sky_count, depth_count, slots),
        out_shape=jax.ShapeDtypeStruct(positions.shape, f32),
        in_specs=[vmem] + [smem] * 6,
        out_specs=vmem,
        scratch_shapes=[
            pltpu.VMEM((3, cells, LANES), f32),
            pltpu.VMEM((3, cells, LANES), f32),
            pltpu.VMEM((3, ghosts, LANES), f32),
            pltpu.VMEM((3, ghosts, LANES), f32),
            pltpu.VMEM((3, cells, LANES), f32),
            pltpu.VMEM((bins, LANES), f32),
            pltpu.VMEM((bins, LANES), f32),
            pltpu.VMEM((bins, LANES), f32),
            pltpu.VMEM((3, ghosts, LANES), f32),
            pltpu.VMEM((4, 8, 3 * slots, LANES), f32),
            pltpu.VMEM((4, 8, 3 * slots, LANES), f32),
            pltpu.VMEM((4, depth_count, 1, LANES), f32),
            pltpu.VMEM((4, sky_count, 1, LANES), f32),
            pltpu.VMEM((LANES // 2 - 1, FIELDS, cells, LANES), f32),
            pltpu.VMEM((LANES, FIELDS, ghosts, LANES), f32),
            dma((4, 8)),
            dma((4, 8)),
            dma((4, depth_count)),
            dma((4, depth_count)),
            dma((4, sky_count)),
            dma((4, sky_count)),
        ],
        compiler_params=pltpu.CompilerParams(collective_id=0, has_side_effects=True, vmem_limit_bytes=40 * 1024 * 1024),
        name="descent",
    )(
        positions,
        cell_points,
        target_log,
        export_count,
        jnp.transpose(export_cell, (2, 0, 1)),
        jnp.transpose(import_pair, (2, 0, 1)),
        jnp.transpose(import_shift, (0, 3, 1, 2)),
    )


def solution(mesh):
    in_specs = (
        P(None, ("sky", "depth"), None),
        P(("sky", "depth")),
        P(),
        P(("sky", "depth"), None),
        P(("sky", "depth"), None, None),
        P(("sky", "depth"), None, None),
        P(None, ("sky", "depth"), None, None),
    )
    out_specs = P(None, ("sky", "depth"), None)
    run = functools.partial(body, mesh.shape["sky"], mesh.shape["depth"])
    return jax.shard_map(run, mesh=mesh, in_specs=in_specs, out_specs=out_specs, check_vma=False)
```

```python
import functools
import math

import jax
import jax.numpy as jnp
from jax import lax
from jax.experimental import pallas as pl
from jax.experimental.pallas import tpu as pltpu
from jax.sharding import PartitionSpec as P

STEPS = 2
EPS_SQ = 0.0001
INV_WIDTH = 16.0
STEP_SIZE = 0.01
GHOST_UNROLL = 8
SELF_UNROLL = 9
FIELDS = 9
FAR = 10000.0
LANES = 128
MESH = pl.DeviceIdType.MESH

HALF_ROOT = math.sqrt(0.5)
GROUPS = ((7, 8), (12, 5), (15, 3))
REGIONS = [(a, b) for a in (-1, 0, 1) for b in (-1, 0, 1) if (a, b) != (0, 0)]


def bin_factor(anchor, k):
    return math.exp(sum(anchor - j - 8 for j in range(k)))


def geometry(left, right):
    offs = [left[i] - right[i] for i in range(3)]
    square = offs[0] * offs[0] + offs[1] * offs[1] + (offs[2] * offs[2] + EPS_SQ)
    inverse = lax.rsqrt(square)
    scaled = (square * inverse) * (INV_WIDTH * HALF_ROOT)
    anchors = []
    for anchor, _ in GROUPS:
        gap = scaled - HALF_ROOT * (anchor + 0.5)
        anchors.append(jnp.exp(-(gap * gap)))
    ratio = jnp.exp(8.0 - scaled * (1.0 / HALF_ROOT))
    return offs + [inverse, scaled, ratio] + anchors


def fold(value):
    total = value[0:8]
    for start in range(8, value.shape[0], 8):
        total = total + value[start : start + 8]
    return total


def add_counts(sums, fields):
    ratio = fields[5]
    anchors = fields[6:]
    sums = list(sums)
    for (anchor, members), term in zip(GROUPS, anchors):
        for k in range(members):
            if k:
                term = term * ratio
            sums[anchor - k] = sums[anchor - k] + fold(term)
    return tuple(sums)


def pair_force(fields, slope, extra):
    offs = fields[:3]
    inverse, scaled, ratio = fields[3:6]
    anchors = fields[6:]
    first = None
    second = None
    for (anchor, members), term in zip(GROUPS, anchors):
        poly = slope(anchor - members + 1)
        poly_extra = extra(anchor - members + 1)
        for k in range(members - 2, -1, -1):
            poly = poly * ratio + slope(anchor - k)
            poly_extra = poly_extra * ratio + extra(anchor - k)
        poly = poly * term
        poly_extra = poly_extra * term
        first = poly if first is None else first + poly
        second = poly_extra if second is None else second + poly_extra
    strength = (scaled * first - second) * inverse
    return [strength * off for off in offs]


def kernel(
    sky_count, depth_count, slots,
    pos_ref, points_ref, target_ref, ecount_ref, ecell_ref, ipair_ref, ishift_ref,
    out_ref,
    cl, cr, lg, rg, grad, work, coef, coef_x, row_grad,
    snd, rcv, ar_rows, self_fields, ghost_fields,
    snd_sem, rcv_sem, ar_send, ar_recv,
):
    bins = 16
    cells = pos_ref.shape[1]
    ghosts = 8 * slots
    sky = lax.axis_index("sky")
    depth = lax.axis_index("depth")
    device_count = sky_count * depth_count
    me = sky * depth_count + depth

    near = []
    for across, along in REGIONS:
        there_sky = lax.rem(sky + across + sky_count, sky_count)
        there_depth = depth + along
        clamped = jnp.clip(there_depth, 0, depth_count - 1)
        if along == 0:
            valid = None
        elif along < 0:
            valid = depth > 0
        else:
            valid = depth < depth_count - 1
        near.append((there_sky, clamped, there_sky * depth_count + clamped, valid))

    def when_valid(valid, action):
        if valid is None:
            action()
        else:
            pl.when(valid)(action)

    barrier = pltpu.get_barrier_semaphore()

    def greet(there_sky, there_depth):
        pl.semaphore_signal(barrier, inc=1, device_id=(there_sky, there_depth), device_id_type=MESH)

    def greet_peer(j, carry):
        peer = lax.rem(me + j, device_count)
        greet(lax.div(peer, depth_count), lax.rem(peer, depth_count))
        return carry

    lax.fori_loop(1, device_count, greet_peer, 0)

    lane = lax.broadcasted_iota(jnp.int32, (1, LANES), 1)
    live_total = jnp.zeros((1, LANES), jnp.float32)
    for c in range(cells):
        live = lane < points_ref[c]
        live_total = live_total + jnp.where(live, 1.0, 0.0)
        x = pos_ref[0, c : c + 1, :]
        cl[0, c : c + 1, :] = jnp.where(live, x, FAR)
        cr[0, c : c + 1, :] = jnp.where(live, x, -FAR)
    for i in (1, 2):
        cl[i] = pos_ref[i]
        cr[i] = pos_ref[i]
    live_total = jnp.sum(live_total, axis=1, keepdims=True)

    for n in range(8):
        nid = near[n][2]
        for k in range(slots):
            cell = ecell_ref[k, 0, nid]
            live = k < ecount_ref[0, nid]
            for i in range(3):
                row = cr[i, pl.ds(cell, 1), :]
                if i == 0:
                    row = jnp.where(live, row, -FAR)
                snd[0, n, i * slots + k : i * slots + k + 1, :] = row

    pl.semaphore_wait(barrier, device_count - 1)

    def message(phase, n):
        there_sky, there_depth, _, _ = near[n]
        return pltpu.make_async_remote_copy(
            src_ref=snd.at[phase, n],
            dst_ref=rcv.at[phase, 7 - n],
            send_sem=snd_sem.at[phase, n],
            recv_sem=rcv_sem.at[phase, 7 - n],
            device_id=(there_sky, there_depth),
            device_id_type=MESH,
        )

    def arrival(phase, n):
        there_sky, there_depth, _, _ = near[n]
        return pltpu.make_async_remote_copy(
            src_ref=snd.at[phase, n],
            dst_ref=rcv.at[phase, n],
            send_sem=snd_sem.at[phase, n],
            recv_sem=rcv_sem.at[phase, n],
            device_id=(there_sky, there_depth),
            device_id_type=MESH,
        )

    def send_all(phase):
        for n in range(8):
            when_valid(near[n][3], lambda n=n: message(phase, n).start())

    def receive_all(phase):
        for n in range(8):
            when_valid(near[n][3], lambda n=n: arrival(phase, n).wait_recv())

    def drain_all(phase):
        for n in range(8):
            when_valid(near[n][3], lambda n=n: message(phase, n).wait_send())

    def all_reduce(phase, row):
        ar_rows[phase, me] = row

        def send(j, carry):
            peer = lax.rem(me + j, device_count)
            pltpu.make_async_remote_copy(
                src_ref=ar_rows.at[phase, me],
                dst_ref=ar_rows.at[phase, me],
                send_sem=ar_send.at[phase],
                recv_sem=ar_recv.at[phase],
                device_id=(lax.div(peer, depth_count), lax.rem(peer, depth_count)),
                device_id_type=MESH,
            ).start()
            return carry

        lax.fori_loop(1, device_count, send, 0)
        others = ar_rows.at[phase, pl.ds(0, device_count - 1)]
        every = pltpu.make_async_remote_copy(
            src_ref=others,
            dst_ref=others,
            send_sem=ar_send.at[phase],
            recv_sem=ar_recv.at[phase],
            device_id=(sky, depth),
            device_id_type=MESH,
        )
        every.wait_recv()
        every.wait_send()
        return jnp.sum(ar_rows[phase], axis=0)

    send_all(0)

    for n in range(8):
        if near[n][3] is not None:

            def fill(n=n):
                for phase in range(4):
                    rcv[phase, n] = jnp.full(rcv.shape[2:], -FAR if phase == 0 else 0.0, jnp.float32)

            pl.when(jnp.logical_not(near[n][3]))(fill)

    def gather_left():
        for n in range(8):
            nid = near[n][2]
            for k in range(slots):
                cell = ipair_ref[k, 0, nid]
                g = n * slots + k
                for i in range(3):
                    shift = ishift_ref[i, k, 0, nid].astype(jnp.float32)
                    lg[i, g : g + 1, :] = cl[i, pl.ds(cell, 1), :] - shift

    def rolled(refs, d):
        back = lax.rem(LANES - d, LANES)
        return [pltpu.roll(refs[i], back, 1) for i in range(3)]

    def rows_of(ref):
        return [ref[i] for i in range(3)]

    def save(ref, at, fields):
        for f, value in enumerate(fields):
            ref[at, f] = value

    def kept(ref, at):
        return [ref[at, f] for f in range(FIELDS)]

    def self_counts():
        left = rows_of(cl)
        right = rows_of(cr)
        zero = tuple(jnp.zeros((8, LANES), jnp.float32) for _ in range(bins))
        ends = add_counts(zero, geometry(left, right))
        ends = add_counts(ends, geometry(left, [pltpu.roll(v, LANES // 2, 1) for v in right]))
        sums = tuple(0.5 * v for v in ends)

        def body(step, sums):
            for j in range(SELF_UNROLL):
                fields = geometry(left, rolled(right, 1 + step * SELF_UNROLL + j))
                save(self_fields, step * SELF_UNROLL + j, fields)
                sums = add_counts(sums, fields)
            return sums

        return lax.fori_loop(0, (LANES // 2 - 1) // SELF_UNROLL, body, sums)

    def ghost_counts(sums):
        def body(step, sums):
            left = rows_of(lg)
            right = rows_of(rg)
            for j in range(GHOST_UNROLL):
                d = step * GHOST_UNROLL + j
                fields = geometry(left, rolled(right, d))
                save(ghost_fields, d, fields)
                sums = add_counts(sums, fields)
            return sums

        return lax.fori_loop(0, LANES // GHOST_UNROLL, body, sums)

    def slope(b):
        return coef[b : b + 1, :]

    def extra(b):
        return coef_x[b : b + 1, :]

    def ghost_forces():
        zero = tuple(jnp.zeros((ghosts, LANES), jnp.float32) for _ in range(6))

        def body(step, sums):
            for j in range(GHOST_UNROLL):
                d = step * GHOST_UNROLL + j
                force = pair_force(kept(ghost_fields, d), slope, extra)
                to_left = tuple(sums[i] + force[i] for i in range(3))
                to_right = tuple(sums[3 + i] - pltpu.roll(force[i], d, 1) for i in range(3))
                sums = to_left + to_right
            return sums

        return lax.fori_loop(0, LANES // GHOST_UNROLL, body, zero)

    def self_forces():
        left = rows_of(cl)
        right = rows_of(cr)
        half = pair_force(geometry(left, [pltpu.roll(v, LANES // 2, 1) for v in right]), slope, extra)

        def body(step, sums):
            for j in range(SELF_UNROLL):
                d = 1 + step * SELF_UNROLL + j
                force = pair_force(kept(self_fields, d - 1), slope, extra)
                sums = tuple(sums[i] + force[i] - pltpu.roll(force[i], d, 1) for i in range(3))
            return sums

        return lax.fori_loop(0, (LANES // 2 - 1) // SELF_UNROLL, body, tuple(half))

    cell_rows = lax.broadcasted_iota(jnp.int32, (cells, LANES), 0)

    def scatter(total, row, cell):
        chosen = cell_rows == cell
        return [total[i] + jnp.where(chosen, row(i), 0.0) for i in range(3)]

    bin_rows = lax.broadcasted_iota(jnp.int32, (bins, LANES), 0)
    bin_lanes = lax.broadcasted_iota(jnp.int32, (bins, LANES), 1)
    on_diagonal = bin_rows == bin_lanes
    centre = bin_rows.astype(jnp.float32) + 0.5
    target = jnp.zeros((bins, LANES), jnp.float32)
    factor = jnp.zeros((bins, LANES), jnp.float32)
    for b in range(bins):
        target = jnp.where(bin_rows == b, target_ref[b], target)
    for anchor, members in GROUPS:
        for k in range(members):
            factor = jnp.where(bin_rows == anchor - k, bin_factor(anchor, k), factor)

    for step in range(STEPS):
        sums = self_counts()
        gather_left()
        if step == 0:
            receive_all(0)
            for n in range(8):
                for i in range(3):
                    rg[i, n * slots : (n + 1) * slots, :] = rcv[0, n, i * slots : (i + 1) * slots, :]
        else:
            receive_all(2)
            for n in range(8):
                for i in range(3):
                    moved = -rcv[2, n, i * slots : (i + 1) * slots, :] * inverse_rms
                    here = rg[i, n * slots : (n + 1) * slots, :]
                    rg[i, n * slots : (n + 1) * slots, :] = here + STEP_SIZE * moved
        sums = ghost_counts(sums)
        for b in range(bins):
            work[b : b + 1, :] = jnp.sum(sums[b], axis=0, keepdims=True)
        local = jnp.sum(work[...], axis=1, keepdims=True) * factor
        row = jnp.sum(jnp.where(on_diagonal, local, 0.0), axis=0, keepdims=True)
        row = all_reduce(2 * step, row)
        counts = jnp.sum(jnp.where(on_diagonal, row, 0.0), axis=1, keepdims=True)
        counts = jnp.broadcast_to(counts, (bins, LANES))
        mean_count = jnp.sum(counts, axis=0, keepdims=True) * (1.0 / bins)
        pull = (jnp.log(1.0 + counts) - target) * mean_count / (1.0 + counts)
        scaled_pull = pull * factor * -INV_WIDTH
        coef[...] = scaled_pull * (1.0 / HALF_ROOT)
        coef_x[...] = scaled_pull * centre

        forces = ghost_forces()
        back = 1 if step == 0 else 3
        for i in range(3):
            for n in range(8):
                snd[back, n, i * slots : (i + 1) * slots, :] = forces[3 + i][n * slots : (n + 1) * slots]
            row_grad[i] = forces[i]
        send_all(back)
        total = list(self_forces())
        for n in range(8):
            nid = near[n][2]
            for k in range(slots):
                g = n * slots + k
                total = scatter(total, lambda i: row_grad[i, g : g + 1, :], ipair_ref[k, 0, nid])
        receive_all(back)
        for n in range(8):
            nid = near[n][2]
            for k in range(slots):
                total = scatter(
                    total, lambda i: rcv[back, n, i * slots + k : i * slots + k + 1, :], ecell_ref[k, 0, nid]
                )
        if step + 1 < STEPS:
            for i in range(3):
                grad[i] = total[i]
            for n in range(8):
                nid = near[n][2]
                for k in range(slots):
                    cell = ecell_ref[k, 0, nid]
                    for i in range(3):
                        snd[2, n, i * slots + k : i * slots + k + 1, :] = grad[i, pl.ds(cell, 1), :]
            send_all(2)
        power = total[0] * total[0] + total[1] * total[1] + total[2] * total[2]
        power = jnp.sum(jnp.sum(power, axis=0, keepdims=True), axis=1, keepdims=True)
        row = jnp.where(lane == 0, power, jnp.where(lane == 1, live_total, 0.0))
        row = all_reduce(2 * step + 1, row)
        power = jnp.sum(jnp.where(lane == 0, row, 0.0), axis=1, keepdims=True)
        live_all = jnp.sum(jnp.where(lane == 1, row, 0.0), axis=1, keepdims=True)
        inverse_rms = 1.0 / jnp.sqrt(power / (3.0 * live_all) + 1e-06)
        for i in range(3):
            move = -total[i] * inverse_rms
            if step == 0:
                out_ref[i] = move
            else:
                out_ref[i] = out_ref[i] + move
            if step + 1 < STEPS:
                cl[i] = cl[i] + STEP_SIZE * move
                cr[i] = cr[i] + STEP_SIZE * move

    for phase in range(4):
        drain_all(phase)


def body(sky_count, depth_count, positions, cell_points, target_log, export_count, export_cell, import_pair, import_shift):
    cells = positions.shape[1]
    slots = export_cell.shape[2]
    bins = target_log.shape[0]
    ghosts = 8 * slots
    vmem = pl.BlockSpec(memory_space=pltpu.VMEM)
    smem = pl.BlockSpec(memory_space=pltpu.SMEM)
    f32 = jnp.float32
    dma = pltpu.SemaphoreType.DMA
    return pl.pallas_call(
        functools.partial(kernel, sky_count, depth_count, slots),
        out_shape=jax.ShapeDtypeStruct(positions.shape, f32),
        in_specs=[vmem] + [smem] * 6,
        out_specs=vmem,
        scratch_shapes=[
            pltpu.VMEM((3, cells, LANES), f32),
            pltpu.VMEM((3, cells, LANES), f32),
            pltpu.VMEM((3, ghosts, LANES), f32),
            pltpu.VMEM((3, ghosts, LANES), f32),
            pltpu.VMEM((3, cells, LANES), f32),
            pltpu.VMEM((bins, LANES), f32),
            pltpu.VMEM((bins, LANES), f32),
            pltpu.VMEM((bins, LANES), f32),
            pltpu.VMEM((3, ghosts, LANES), f32),
            pltpu.VMEM((4, 8, 3 * slots, LANES), f32),
            pltpu.VMEM((4, 8, 3 * slots, LANES), f32),
            pltpu.VMEM((4, sky_count * depth_count, 1, LANES), f32),
            pltpu.VMEM((LANES // 2 - 1, FIELDS, cells, LANES), f32),
            pltpu.VMEM((LANES, FIELDS, ghosts, LANES), f32),
            dma((4, 8)),
            dma((4, 8)),
            dma((4,)),
            dma((4,)),
        ],
        compiler_params=pltpu.CompilerParams(collective_id=0, has_side_effects=True, vmem_limit_bytes=40 * 1024 * 1024),
        name="descent",
    )(
        positions,
        cell_points,
        target_log,
        export_count,
        jnp.transpose(export_cell, (2, 0, 1)),
        jnp.transpose(import_pair, (2, 0, 1)),
        jnp.transpose(import_shift, (0, 3, 1, 2)),
    )


def solution(mesh):
    in_specs = (
        P(None, ("sky", "depth"), None),
        P(("sky", "depth")),
        P(),
        P(("sky", "depth"), None),
        P(("sky", "depth"), None, None),
        P(("sky", "depth"), None, None),
        P(None, ("sky", "depth"), None, None),
    )
    out_specs = P(None, ("sky", "depth"), None)
    run = functools.partial(body, mesh.shape["sky"], mesh.shape["depth"])
    return jax.shard_map(run, mesh=mesh, in_specs=in_specs, out_specs=out_specs, check_vma=False)
```

```python
import functools
import math

import jax
import jax.numpy as jnp
from jax import lax
from jax.experimental import pallas as pl
from jax.experimental.pallas import tpu as pltpu
from jax.sharding import PartitionSpec as P

STEPS = 2
EPS_SQ = 0.0001
INV_WIDTH = 16.0
STEP_SIZE = 0.01
GHOST_UNROLL = 16
SELF_UNROLL = 21
FIELDS = 9
FAR = 10000.0
LANES = 128
MESH = pl.DeviceIdType.MESH

HALF_ROOT = math.sqrt(0.5)
GROUPS = ((7, 8), (12, 5), (15, 3))
REGIONS = [(a, b) for a in (-1, 0, 1) for b in (-1, 0, 1) if (a, b) != (0, 0)]


def bin_factor(anchor, k):
    return math.exp(sum(anchor - j - 8 for j in range(k)))


def geometry(left, right):
    offs = [left[i] - right[i] for i in range(3)]
    square = offs[0] * offs[0] + offs[1] * offs[1] + (offs[2] * offs[2] + EPS_SQ)
    inverse = lax.rsqrt(square)
    scaled = (square * inverse) * (INV_WIDTH * HALF_ROOT)
    anchors = []
    for anchor, _ in GROUPS:
        gap = scaled - HALF_ROOT * (anchor + 0.5)
        anchors.append(jnp.exp(-(gap * gap)))
    ratio = jnp.exp(8.0 - scaled * (1.0 / HALF_ROOT))
    return offs + [inverse, scaled, ratio] + anchors


def fold(value):
    total = value[0:8]
    for start in range(8, value.shape[0], 8):
        total = total + value[start : start + 8]
    return total


def add_counts(sums, fields):
    ratio = fields[5]
    anchors = fields[6:]
    sums = list(sums)
    for (anchor, members), term in zip(GROUPS, anchors):
        for k in range(members):
            if k:
                term = term * ratio
            sums[anchor - k] = sums[anchor - k] + fold(term)
    return tuple(sums)


def pair_force(fields, slope, extra):
    offs = fields[:3]
    inverse, scaled, ratio = fields[3:6]
    anchors = fields[6:]
    first = None
    second = None
    for (anchor, members), term in zip(GROUPS, anchors):
        poly = slope(anchor - members + 1)
        poly_extra = extra(anchor - members + 1)
        for k in range(members - 2, -1, -1):
            poly = poly * ratio + slope(anchor - k)
            poly_extra = poly_extra * ratio + extra(anchor - k)
        poly = poly * term
        poly_extra = poly_extra * term
        first = poly if first is None else first + poly
        second = poly_extra if second is None else second + poly_extra
    strength = (scaled * first - second) * inverse
    return [strength * off for off in offs]


def kernel(
    sky_count, depth_count, slots,
    pos_ref, points_ref, target_ref, ecount_ref, ecell_ref, ipair_ref, ishift_ref,
    out_ref,
    cl, cr, lg, rg, grad, work, coef, coef_x, row_grad,
    snd, rcv, ar_rows, self_fields, ghost_fields,
    snd_sem, rcv_sem, ar_send, ar_recv,
):
    bins = 16
    cells = pos_ref.shape[1]
    ghosts = 8 * slots
    sky = lax.axis_index("sky")
    depth = lax.axis_index("depth")
    device_count = sky_count * depth_count
    me = sky * depth_count + depth

    near = []
    for across, along in REGIONS:
        there_sky = lax.rem(sky + across + sky_count, sky_count)
        there_depth = depth + along
        clamped = jnp.clip(there_depth, 0, depth_count - 1)
        if along == 0:
            valid = None
        elif along < 0:
            valid = depth > 0
        else:
            valid = depth < depth_count - 1
        near.append((there_sky, clamped, there_sky * depth_count + clamped, valid))

    def when_valid(valid, action):
        if valid is None:
            action()
        else:
            pl.when(valid)(action)

    barrier = pltpu.get_barrier_semaphore()

    def greet(there_sky, there_depth):
        pl.semaphore_signal(barrier, inc=1, device_id=(there_sky, there_depth), device_id_type=MESH)

    def greet_peer(j, carry):
        peer = lax.rem(me + j, device_count)
        greet(lax.div(peer, depth_count), lax.rem(peer, depth_count))
        return carry

    lax.fori_loop(1, device_count, greet_peer, 0)

    lane = lax.broadcasted_iota(jnp.int32, (1, LANES), 1)
    live_total = jnp.zeros((1, LANES), jnp.float32)
    for c in range(cells):
        live = lane < points_ref[c]
        live_total = live_total + jnp.where(live, 1.0, 0.0)
        x = pos_ref[0, c : c + 1, :]
        cl[0, c : c + 1, :] = jnp.where(live, x, FAR)
        cr[0, c : c + 1, :] = jnp.where(live, x, -FAR)
    for i in (1, 2):
        cl[i] = pos_ref[i]
        cr[i] = pos_ref[i]
    live_total = jnp.sum(live_total, axis=1, keepdims=True)

    for n in range(8):
        nid = near[n][2]
        for k in range(slots):
            cell = ecell_ref[k, 0, nid]
            live = k < ecount_ref[0, nid]
            for i in range(3):
                row = cr[i, pl.ds(cell, 1), :]
                if i == 0:
                    row = jnp.where(live, row, -FAR)
                snd[0, n, i * slots + k : i * slots + k + 1, :] = row

    pl.semaphore_wait(barrier, device_count - 1)

    def message(phase, n):
        there_sky, there_depth, _, _ = near[n]
        return pltpu.make_async_remote_copy(
            src_ref=snd.at[phase, n],
            dst_ref=rcv.at[phase, 7 - n],
            send_sem=snd_sem.at[phase, n],
            recv_sem=rcv_sem.at[phase, 7 - n],
            device_id=(there_sky, there_depth),
            device_id_type=MESH,
        )

    def arrival(phase, n):
        there_sky, there_depth, _, _ = near[n]
        return pltpu.make_async_remote_copy(
            src_ref=snd.at[phase, n],
            dst_ref=rcv.at[phase, n],
            send_sem=snd_sem.at[phase, n],
            recv_sem=rcv_sem.at[phase, n],
            device_id=(there_sky, there_depth),
            device_id_type=MESH,
        )

    def send_all(phase):
        for n in range(8):
            when_valid(near[n][3], lambda n=n: message(phase, n).start())

    def receive_all(phase):
        for n in range(8):
            when_valid(near[n][3], lambda n=n: arrival(phase, n).wait_recv())

    def drain_all(phase):
        for n in range(8):
            when_valid(near[n][3], lambda n=n: message(phase, n).wait_send())

    def all_reduce(phase, row):
        ar_rows[phase, me] = row

        def send(j, carry):
            peer = lax.rem(me + j, device_count)
            pltpu.make_async_remote_copy(
                src_ref=ar_rows.at[phase, me],
                dst_ref=ar_rows.at[phase, me],
                send_sem=ar_send.at[phase],
                recv_sem=ar_recv.at[phase],
                device_id=(lax.div(peer, depth_count), lax.rem(peer, depth_count)),
                device_id_type=MESH,
            ).start()
            return carry

        lax.fori_loop(1, device_count, send, 0)
        others = ar_rows.at[phase, pl.ds(0, device_count - 1)]
        every = pltpu.make_async_remote_copy(
            src_ref=others,
            dst_ref=others,
            send_sem=ar_send.at[phase],
            recv_sem=ar_recv.at[phase],
            device_id=(sky, depth),
            device_id_type=MESH,
        )
        every.wait_recv()
        every.wait_send()
        return jnp.sum(ar_rows[phase], axis=0)

    send_all(0)

    for n in range(8):
        if near[n][3] is not None:

            def fill(n=n):
                for phase in range(4):
                    rcv[phase, n] = jnp.full(rcv.shape[2:], -FAR if phase == 0 else 0.0, jnp.float32)

            pl.when(jnp.logical_not(near[n][3]))(fill)

    def gather_left():
        for n in range(8):
            nid = near[n][2]
            for k in range(slots):
                cell = ipair_ref[k, 0, nid]
                g = n * slots + k
                for i in range(3):
                    shift = ishift_ref[i, k, 0, nid].astype(jnp.float32)
                    lg[i, g : g + 1, :] = cl[i, pl.ds(cell, 1), :] - shift

    def rolled(refs, d):
        back = lax.rem(LANES - d, LANES)
        return [pltpu.roll(refs[i], back, 1) for i in range(3)]

    def rows_of(ref):
        return [ref[i] for i in range(3)]

    def save(ref, at, fields):
        for f, value in enumerate(fields):
            ref[at, f] = value

    def kept(ref, at):
        return [ref[at, f] for f in range(FIELDS)]

    def self_counts():
        left = rows_of(cl)
        right = rows_of(cr)
        zero = tuple(jnp.zeros((8, LANES), jnp.float32) for _ in range(bins))
        ends = add_counts(zero, geometry(left, right))
        ends = add_counts(ends, geometry(left, [pltpu.roll(v, LANES // 2, 1) for v in right]))
        sums = tuple(0.5 * v for v in ends)

        def body(step, sums):
            for j in range(SELF_UNROLL):
                fields = geometry(left, rolled(right, 1 + step * SELF_UNROLL + j))
                save(self_fields, step * SELF_UNROLL + j, fields)
                sums = add_counts(sums, fields)
            return sums

        return lax.fori_loop(0, (LANES // 2 - 1) // SELF_UNROLL, body, sums)

    def ghost_counts(sums):
        def body(step, sums):
            left = rows_of(lg)
            right = rows_of(rg)
            for j in range(GHOST_UNROLL):
                d = step * GHOST_UNROLL + j
                fields = geometry(left, rolled(right, d))
                save(ghost_fields, d, fields)
                sums = add_counts(sums, fields)
            return sums

        return lax.fori_loop(0, LANES // GHOST_UNROLL, body, sums)

    def slope(b):
        return coef[b : b + 1, :]

    def extra(b):
        return coef_x[b : b + 1, :]

    def ghost_forces():
        zero = tuple(jnp.zeros((ghosts, LANES), jnp.float32) for _ in range(6))

        def body(step, sums):
            for j in range(GHOST_UNROLL):
                d = step * GHOST_UNROLL + j
                force = pair_force(kept(ghost_fields, d), slope, extra)
                to_left = tuple(sums[i] + force[i] for i in range(3))
                to_right = tuple(sums[3 + i] - pltpu.roll(force[i], d, 1) for i in range(3))
                sums = to_left + to_right
            return sums

        return lax.fori_loop(0, LANES // GHOST_UNROLL, body, zero)

    def self_forces():
        left = rows_of(cl)
        right = rows_of(cr)
        half = pair_force(geometry(left, [pltpu.roll(v, LANES // 2, 1) for v in right]), slope, extra)

        def body(step, sums):
            for j in range(SELF_UNROLL):
                d = 1 + step * SELF_UNROLL + j
                force = pair_force(kept(self_fields, d - 1), slope, extra)
                sums = tuple(sums[i] + force[i] - pltpu.roll(force[i], d, 1) for i in range(3))
            return sums

        return lax.fori_loop(0, (LANES // 2 - 1) // SELF_UNROLL, body, tuple(half))

    cell_rows = lax.broadcasted_iota(jnp.int32, (cells, LANES), 0)

    def scatter(total, row, cell):
        chosen = cell_rows == cell
        return [total[i] + jnp.where(chosen, row(i), 0.0) for i in range(3)]

    bin_rows = lax.broadcasted_iota(jnp.int32, (bins, LANES), 0)
    bin_lanes = lax.broadcasted_iota(jnp.int32, (bins, LANES), 1)
    on_diagonal = bin_rows == bin_lanes
    centre = bin_rows.astype(jnp.float32) + 0.5
    target = jnp.zeros((bins, LANES), jnp.float32)
    factor = jnp.zeros((bins, LANES), jnp.float32)
    for b in range(bins):
        target = jnp.where(bin_rows == b, target_ref[b], target)
    for anchor, members in GROUPS:
        for k in range(members):
            factor = jnp.where(bin_rows == anchor - k, bin_factor(anchor, k), factor)

    for step in range(STEPS):
        sums = self_counts()
        gather_left()
        if step == 0:
            receive_all(0)
            for n in range(8):
                for i in range(3):
                    rg[i, n * slots : (n + 1) * slots, :] = rcv[0, n, i * slots : (i + 1) * slots, :]
        else:
            receive_all(2)
            for n in range(8):
                for i in range(3):
                    moved = -rcv[2, n, i * slots : (i + 1) * slots, :] * inverse_rms
                    here = rg[i, n * slots : (n + 1) * slots, :]
                    rg[i, n * slots : (n + 1) * slots, :] = here + STEP_SIZE * moved
        sums = ghost_counts(sums)
        for b in range(bins):
            work[b : b + 1, :] = jnp.sum(sums[b], axis=0, keepdims=True)
        local = jnp.sum(work[...], axis=1, keepdims=True) * factor
        row = jnp.sum(jnp.where(on_diagonal, local, 0.0), axis=0, keepdims=True)
        row = all_reduce(2 * step, row)
        counts = jnp.sum(jnp.where(on_diagonal, row, 0.0), axis=1, keepdims=True)
        counts = jnp.broadcast_to(counts, (bins, LANES))
        mean_count = jnp.sum(counts, axis=0, keepdims=True) * (1.0 / bins)
        pull = (jnp.log(1.0 + counts) - target) * mean_count / (1.0 + counts)
        scaled_pull = pull * factor * -INV_WIDTH
        coef[...] = scaled_pull * (1.0 / HALF_ROOT)
        coef_x[...] = scaled_pull * centre

        forces = ghost_forces()
        back = 1 if step == 0 else 3
        for i in range(3):
            for n in range(8):
                snd[back, n, i * slots : (i + 1) * slots, :] = forces[3 + i][n * slots : (n + 1) * slots]
            row_grad[i] = forces[i]
        send_all(back)
        total = list(self_forces())
        for n in range(8):
            nid = near[n][2]
            for k in range(slots):
                g = n * slots + k
                total = scatter(total, lambda i: row_grad[i, g : g + 1, :], ipair_ref[k, 0, nid])
        receive_all(back)
        for n in range(8):
            nid = near[n][2]
            for k in range(slots):
                total = scatter(
                    total, lambda i: rcv[back, n, i * slots + k : i * slots + k + 1, :], ecell_ref[k, 0, nid]
                )
        if step + 1 < STEPS:
            for i in range(3):
                grad[i] = total[i]
            for n in range(8):
                nid = near[n][2]
                for k in range(slots):
                    cell = ecell_ref[k, 0, nid]
                    for i in range(3):
                        snd[2, n, i * slots + k : i * slots + k + 1, :] = grad[i, pl.ds(cell, 1), :]
            send_all(2)
        power = total[0] * total[0] + total[1] * total[1] + total[2] * total[2]
        power = jnp.sum(jnp.sum(power, axis=0, keepdims=True), axis=1, keepdims=True)
        row = jnp.where(lane == 0, power, jnp.where(lane == 1, live_total, 0.0))
        row = all_reduce(2 * step + 1, row)
        power = jnp.sum(jnp.where(lane == 0, row, 0.0), axis=1, keepdims=True)
        live_all = jnp.sum(jnp.where(lane == 1, row, 0.0), axis=1, keepdims=True)
        inverse_rms = 1.0 / jnp.sqrt(power / (3.0 * live_all) + 1e-06)
        for i in range(3):
            move = -total[i] * inverse_rms
            if step == 0:
                out_ref[i] = move
            else:
                out_ref[i] = out_ref[i] + move
            if step + 1 < STEPS:
                cl[i] = cl[i] + STEP_SIZE * move
                cr[i] = cr[i] + STEP_SIZE * move

    for phase in range(4):
        drain_all(phase)


def body(sky_count, depth_count, positions, cell_points, target_log, export_count, export_cell, import_pair, import_shift):
    cells = positions.shape[1]
    slots = export_cell.shape[2]
    bins = target_log.shape[0]
    ghosts = 8 * slots
    vmem = pl.BlockSpec(memory_space=pltpu.VMEM)
    smem = pl.BlockSpec(memory_space=pltpu.SMEM)
    f32 = jnp.float32
    dma = pltpu.SemaphoreType.DMA
    return pl.pallas_call(
        functools.partial(kernel, sky_count, depth_count, slots),
        out_shape=jax.ShapeDtypeStruct(positions.shape, f32),
        in_specs=[vmem] + [smem] * 6,
        out_specs=vmem,
        scratch_shapes=[
            pltpu.VMEM((3, cells, LANES), f32),
            pltpu.VMEM((3, cells, LANES), f32),
            pltpu.VMEM((3, ghosts, LANES), f32),
            pltpu.VMEM((3, ghosts, LANES), f32),
            pltpu.VMEM((3, cells, LANES), f32),
            pltpu.VMEM((bins, LANES), f32),
            pltpu.VMEM((bins, LANES), f32),
            pltpu.VMEM((bins, LANES), f32),
            pltpu.VMEM((3, ghosts, LANES), f32),
            pltpu.VMEM((4, 8, 3 * slots, LANES), f32),
            pltpu.VMEM((4, 8, 3 * slots, LANES), f32),
            pltpu.VMEM((4, sky_count * depth_count, 1, LANES), f32),
            pltpu.VMEM((LANES // 2 - 1, FIELDS, cells, LANES), f32),
            pltpu.VMEM((LANES, FIELDS, ghosts, LANES), f32),
            dma((4, 8)),
            dma((4, 8)),
            dma((4,)),
            dma((4,)),
        ],
        compiler_params=pltpu.CompilerParams(collective_id=0, has_side_effects=True, vmem_limit_bytes=40 * 1024 * 1024),
        name="descent",
    )(
        positions,
        cell_points,
        target_log,
        export_count,
        jnp.transpose(export_cell, (2, 0, 1)),
        jnp.transpose(import_pair, (2, 0, 1)),
        jnp.transpose(import_shift, (0, 3, 1, 2)),
    )


def solution(mesh):
    in_specs = (
        P(None, ("sky", "depth"), None),
        P(("sky", "depth")),
        P(),
        P(("sky", "depth"), None),
        P(("sky", "depth"), None, None),
        P(("sky", "depth"), None, None),
        P(None, ("sky", "depth"), None, None),
    )
    out_specs = P(None, ("sky", "depth"), None)
    run = functools.partial(body, mesh.shape["sky"], mesh.shape["depth"])
    return jax.shard_map(run, mesh=mesh, in_specs=in_specs, out_specs=out_specs, check_vma=False)
```

```python
import functools
import math

import jax
import jax.numpy as jnp
from jax import lax
from jax.experimental import pallas as pl
from jax.experimental.pallas import tpu as pltpu
from jax.sharding import PartitionSpec as P

STEPS = 2
EPS_SQ = 0.0001
INV_WIDTH = 16.0
STEP_SIZE = 0.01
GHOST_UNROLL = 16
SELF_UNROLL = 9
FORCE_UNROLL = 8
FIELDS = 9
FAR = 10000.0
LANES = 128
MESH = pl.DeviceIdType.MESH

HALF_ROOT = math.sqrt(0.5)
GROUPS = ((7, 8), (12, 5), (15, 3))
REGIONS = [(a, b) for a in (-1, 0, 1) for b in (-1, 0, 1) if (a, b) != (0, 0)]


def bin_factor(anchor, k):
    return math.exp(sum(anchor - j - 8 for j in range(k)))


def geometry(left, right):
    offs = [left[i] - right[i] for i in range(3)]
    square = offs[0] * offs[0] + offs[1] * offs[1] + (offs[2] * offs[2] + EPS_SQ)
    inverse = lax.rsqrt(square)
    scaled = (square * inverse) * (INV_WIDTH * HALF_ROOT)
    anchors = []
    for anchor, _ in GROUPS:
        gap = scaled - HALF_ROOT * (anchor + 0.5)
        anchors.append(jnp.exp(-(gap * gap)))
    ratio = jnp.exp(8.0 - scaled * (1.0 / HALF_ROOT))
    return offs + [inverse, scaled, ratio] + anchors


def fold(value):
    total = value[0:8]
    for start in range(8, value.shape[0], 8):
        total = total + value[start : start + 8]
    return total


def add_counts(sums, fields):
    ratio = fields[5]
    anchors = fields[6:]
    sums = list(sums)
    for (anchor, members), term in zip(GROUPS, anchors):
        for k in range(members):
            if k:
                term = term * ratio
            sums[anchor - k] = sums[anchor - k] + fold(term)
    return tuple(sums)


def pair_force(fields, slope, extra):
    offs = fields[:3]
    inverse, scaled, ratio = fields[3:6]
    anchors = fields[6:]
    first = None
    second = None
    for (anchor, members), term in zip(GROUPS, anchors):
        poly = slope(anchor - members + 1)
        poly_extra = extra(anchor - members + 1)
        for k in range(members - 2, -1, -1):
            poly = poly * ratio + slope(anchor - k)
            poly_extra = poly_extra * ratio + extra(anchor - k)
        poly = poly * term
        poly_extra = poly_extra * term
        first = poly if first is None else first + poly
        second = poly_extra if second is None else second + poly_extra
    strength = (scaled * first - second) * inverse
    return [strength * off for off in offs]


def kernel(
    sky_count, depth_count, slots,
    pos_ref, points_ref, target_ref, ecount_ref, ecell_ref, ipair_ref, ishift_ref,
    out_ref,
    cl, cr, lg, rg, grad, work, coef, coef_x, row_grad,
    snd, rcv, ar_rows, self_fields, ghost_fields,
    snd_sem, rcv_sem, ar_send, ar_recv,
):
    bins = 16
    cells = pos_ref.shape[1]
    ghosts = 8 * slots
    sky = lax.axis_index("sky")
    depth = lax.axis_index("depth")
    device_count = sky_count * depth_count
    me = sky * depth_count + depth

    near = []
    for across, along in REGIONS:
        there_sky = lax.rem(sky + across + sky_count, sky_count)
        there_depth = depth + along
        clamped = jnp.clip(there_depth, 0, depth_count - 1)
        if along == 0:
            valid = None
        elif along < 0:
            valid = depth > 0
        else:
            valid = depth < depth_count - 1
        near.append((there_sky, clamped, there_sky * depth_count + clamped, valid))

    def when_valid(valid, action):
        if valid is None:
            action()
        else:
            pl.when(valid)(action)

    barrier = pltpu.get_barrier_semaphore()

    def greet(there_sky, there_depth):
        pl.semaphore_signal(barrier, inc=1, device_id=(there_sky, there_depth), device_id_type=MESH)

    def greet_peer(j, carry):
        peer = lax.rem(me + j, device_count)
        greet(lax.div(peer, depth_count), lax.rem(peer, depth_count))
        return carry

    lax.fori_loop(1, device_count, greet_peer, 0)

    lane = lax.broadcasted_iota(jnp.int32, (1, LANES), 1)
    live_total = jnp.zeros((1, LANES), jnp.float32)
    for c in range(cells):
        live = lane < points_ref[c]
        live_total = live_total + jnp.where(live, 1.0, 0.0)
        x = pos_ref[0, c : c + 1, :]
        cl[0, c : c + 1, :] = jnp.where(live, x, FAR)
        cr[0, c : c + 1, :] = jnp.where(live, x, -FAR)
    for i in (1, 2):
        cl[i] = pos_ref[i]
        cr[i] = pos_ref[i]
    live_total = jnp.sum(live_total, axis=1, keepdims=True)

    for n in range(8):
        nid = near[n][2]
        for k in range(slots):
            cell = ecell_ref[k, 0, nid]
            live = k < ecount_ref[0, nid]
            for i in range(3):
                row = cr[i, pl.ds(cell, 1), :]
                if i == 0:
                    row = jnp.where(live, row, -FAR)
                snd[0, n, i * slots + k : i * slots + k + 1, :] = row

    pl.semaphore_wait(barrier, device_count - 1)

    def message(phase, n):
        there_sky, there_depth, _, _ = near[n]
        return pltpu.make_async_remote_copy(
            src_ref=snd.at[phase, n],
            dst_ref=rcv.at[phase, 7 - n],
            send_sem=snd_sem.at[phase, n],
            recv_sem=rcv_sem.at[phase, 7 - n],
            device_id=(there_sky, there_depth),
            device_id_type=MESH,
        )

    def arrival(phase, n):
        there_sky, there_depth, _, _ = near[n]
        return pltpu.make_async_remote_copy(
            src_ref=snd.at[phase, n],
            dst_ref=rcv.at[phase, n],
            send_sem=snd_sem.at[phase, n],
            recv_sem=rcv_sem.at[phase, n],
            device_id=(there_sky, there_depth),
            device_id_type=MESH,
        )

    def send_all(phase):
        for n in range(8):
            when_valid(near[n][3], lambda n=n: message(phase, n).start())

    def receive_all(phase):
        for n in range(8):
            when_valid(near[n][3], lambda n=n: arrival(phase, n).wait_recv())

    def drain_all(phase):
        for n in range(8):
            when_valid(near[n][3], lambda n=n: message(phase, n).wait_send())

    def all_reduce(phase, row):
        ar_rows[phase, me] = row

        for a in range(sky_count):
            for b in range(depth_count):
                if (a, b) != (0, 0):
                    pltpu.make_async_remote_copy(
                        src_ref=ar_rows.at[phase, me],
                        dst_ref=ar_rows.at[phase, me],
                        send_sem=ar_send.at[phase],
                        recv_sem=ar_recv.at[phase],
                        device_id=(lax.rem(sky + a, sky_count), lax.rem(depth + b, depth_count)),
                        device_id_type=MESH,
                    ).start()
        others = ar_rows.at[phase, pl.ds(0, device_count - 1)]
        every = pltpu.make_async_remote_copy(
            src_ref=others,
            dst_ref=others,
            send_sem=ar_send.at[phase],
            recv_sem=ar_recv.at[phase],
            device_id=(sky, depth),
            device_id_type=MESH,
        )
        every.wait_recv()
        every.wait_send()
        return jnp.sum(ar_rows[phase], axis=0)

    send_all(0)

    for n in range(8):
        if near[n][3] is not None:

            def fill(n=n):
                for phase in range(4):
                    rcv[phase, n] = jnp.full(rcv.shape[2:], -FAR if phase == 0 else 0.0, jnp.float32)

            pl.when(jnp.logical_not(near[n][3]))(fill)

    def gather_left():
        for n in range(8):
            nid = near[n][2]
            for k in range(slots):
                cell = ipair_ref[k, 0, nid]
                g = n * slots + k
                for i in range(3):
                    shift = ishift_ref[i, k, 0, nid].astype(jnp.float32)
                    lg[i, g : g + 1, :] = cl[i, pl.ds(cell, 1), :] - shift

    def rolled(refs, d):
        back = lax.rem(LANES - d, LANES)
        return [pltpu.roll(refs[i], back, 1) for i in range(3)]

    def rows_of(ref):
        return [ref[i] for i in range(3)]

    def save(ref, at, fields):
        for f, value in enumerate(fields):
            ref[at, f] = value

    def kept(ref, at):
        return [ref[at, f] for f in range(FIELDS)]

    def self_counts():
        left = rows_of(cl)
        right = rows_of(cr)
        zero = tuple(jnp.zeros((8, LANES), jnp.float32) for _ in range(bins))
        ends = add_counts(zero, geometry(left, right))
        ends = add_counts(ends, geometry(left, [pltpu.roll(v, LANES // 2, 1) for v in right]))
        sums = tuple(0.5 * v for v in ends)

        def body(step, sums):
            for j in range(SELF_UNROLL):
                fields = geometry(left, rolled(right, 1 + step * SELF_UNROLL + j))
                save(self_fields, step * SELF_UNROLL + j, fields)
                sums = add_counts(sums, fields)
            return sums

        return lax.fori_loop(0, (LANES // 2 - 1) // SELF_UNROLL, body, sums)

    def ghost_counts(sums):
        def body(step, sums):
            left = rows_of(lg)
            right = rows_of(rg)
            for j in range(GHOST_UNROLL):
                d = step * GHOST_UNROLL + j
                fields = geometry(left, rolled(right, d))
                save(ghost_fields, d, fields)
                sums = add_counts(sums, fields)
            return sums

        return lax.fori_loop(0, LANES // GHOST_UNROLL, body, sums)

    def slope(b):
        return coef[b : b + 1, :]

    def extra(b):
        return coef_x[b : b + 1, :]

    def ghost_forces():
        zero = tuple(jnp.zeros((ghosts, LANES), jnp.float32) for _ in range(6))

        def body(step, sums):
            for j in range(FORCE_UNROLL):
                d = step * FORCE_UNROLL + j
                force = pair_force(kept(ghost_fields, d), slope, extra)
                to_left = tuple(sums[i] + force[i] for i in range(3))
                to_right = tuple(sums[3 + i] - pltpu.roll(force[i], d, 1) for i in range(3))
                sums = to_left + to_right
            return sums

        return lax.fori_loop(0, LANES // FORCE_UNROLL, body, zero)

    def self_forces():
        left = rows_of(cl)
        right = rows_of(cr)
        half = pair_force(geometry(left, [pltpu.roll(v, LANES // 2, 1) for v in right]), slope, extra)

        def body(step, sums):
            for j in range(SELF_UNROLL):
                d = 1 + step * SELF_UNROLL + j
                force = pair_force(kept(self_fields, d - 1), slope, extra)
                sums = tuple(sums[i] + force[i] - pltpu.roll(force[i], d, 1) for i in range(3))
            return sums

        return lax.fori_loop(0, (LANES // 2 - 1) // SELF_UNROLL, body, tuple(half))

    cell_rows = lax.broadcasted_iota(jnp.int32, (cells, LANES), 0)

    def scatter(total, row, cell):
        chosen = cell_rows == cell
        return [total[i] + jnp.where(chosen, row(i), 0.0) for i in range(3)]

    bin_rows = lax.broadcasted_iota(jnp.int32, (bins, LANES), 0)
    bin_lanes = lax.broadcasted_iota(jnp.int32, (bins, LANES), 1)
    on_diagonal = bin_rows == bin_lanes
    centre = bin_rows.astype(jnp.float32) + 0.5
    target = jnp.zeros((bins, LANES), jnp.float32)
    factor = jnp.zeros((bins, LANES), jnp.float32)
    for b in range(bins):
        target = jnp.where(bin_rows == b, target_ref[b], target)
    for anchor, members in GROUPS:
        for k in range(members):
            factor = jnp.where(bin_rows == anchor - k, bin_factor(anchor, k), factor)

    for step in range(STEPS):
        sums = self_counts()
        gather_left()
        if step == 0:
            receive_all(0)
            for n in range(8):
                for i in range(3):
                    rg[i, n * slots : (n + 1) * slots, :] = rcv[0, n, i * slots : (i + 1) * slots, :]
        else:
            receive_all(2)
            for n in range(8):
                for i in range(3):
                    moved = -rcv[2, n, i * slots : (i + 1) * slots, :] * inverse_rms
                    here = rg[i, n * slots : (n + 1) * slots, :]
                    rg[i, n * slots : (n + 1) * slots, :] = here + STEP_SIZE * moved
        sums = ghost_counts(sums)
        for b in range(bins):
            work[b : b + 1, :] = jnp.sum(sums[b], axis=0, keepdims=True)
        local = jnp.sum(work[...], axis=1, keepdims=True) * factor
        row = jnp.sum(jnp.where(on_diagonal, local, 0.0), axis=0, keepdims=True)
        row = all_reduce(2 * step, row)
        counts = jnp.sum(jnp.where(on_diagonal, row, 0.0), axis=1, keepdims=True)
        counts = jnp.broadcast_to(counts, (bins, LANES))
        mean_count = jnp.sum(counts, axis=0, keepdims=True) * (1.0 / bins)
        pull = (jnp.log(1.0 + counts) - target) * mean_count / (1.0 + counts)
        scaled_pull = pull * factor * -INV_WIDTH
        coef[...] = scaled_pull * (1.0 / HALF_ROOT)
        coef_x[...] = scaled_pull * centre

        forces = ghost_forces()
        back = 1 if step == 0 else 3
        for i in range(3):
            for n in range(8):
                snd[back, n, i * slots : (i + 1) * slots, :] = forces[3 + i][n * slots : (n + 1) * slots]
            row_grad[i] = forces[i]
        send_all(back)
        total = list(self_forces())
        for n in range(8):
            nid = near[n][2]
            for k in range(slots):
                g = n * slots + k
                total = scatter(total, lambda i: row_grad[i, g : g + 1, :], ipair_ref[k, 0, nid])
        receive_all(back)
        for n in range(8):
            nid = near[n][2]
            for k in range(slots):
                total = scatter(
                    total, lambda i: rcv[back, n, i * slots + k : i * slots + k + 1, :], ecell_ref[k, 0, nid]
                )
        if step + 1 < STEPS:
            for i in range(3):
                grad[i] = total[i]
            for n in range(8):
                nid = near[n][2]
                for k in range(slots):
                    cell = ecell_ref[k, 0, nid]
                    for i in range(3):
                        snd[2, n, i * slots + k : i * slots + k + 1, :] = grad[i, pl.ds(cell, 1), :]
            send_all(2)
        power = total[0] * total[0] + total[1] * total[1] + total[2] * total[2]
        power = jnp.sum(jnp.sum(power, axis=0, keepdims=True), axis=1, keepdims=True)
        row = jnp.where(lane == 0, power, jnp.where(lane == 1, live_total, 0.0))
        row = all_reduce(2 * step + 1, row)
        power = jnp.sum(jnp.where(lane == 0, row, 0.0), axis=1, keepdims=True)
        live_all = jnp.sum(jnp.where(lane == 1, row, 0.0), axis=1, keepdims=True)
        inverse_rms = 1.0 / jnp.sqrt(power / (3.0 * live_all) + 1e-06)
        for i in range(3):
            move = -total[i] * inverse_rms
            if step == 0:
                out_ref[i] = move
            else:
                out_ref[i] = out_ref[i] + move
            if step + 1 < STEPS:
                cl[i] = cl[i] + STEP_SIZE * move
                cr[i] = cr[i] + STEP_SIZE * move

    for phase in range(4):
        drain_all(phase)


def body(sky_count, depth_count, positions, cell_points, target_log, export_count, export_cell, import_pair, import_shift):
    cells = positions.shape[1]
    slots = export_cell.shape[2]
    bins = target_log.shape[0]
    ghosts = 8 * slots
    vmem = pl.BlockSpec(memory_space=pltpu.VMEM)
    smem = pl.BlockSpec(memory_space=pltpu.SMEM)
    f32 = jnp.float32
    dma = pltpu.SemaphoreType.DMA
    return pl.pallas_call(
        functools.partial(kernel, sky_count, depth_count, slots),
        out_shape=jax.ShapeDtypeStruct(positions.shape, f32),
        in_specs=[vmem] + [smem] * 6,
        out_specs=vmem,
        scratch_shapes=[
            pltpu.VMEM((3, cells, LANES), f32),
            pltpu.VMEM((3, cells, LANES), f32),
            pltpu.VMEM((3, ghosts, LANES), f32),
            pltpu.VMEM((3, ghosts, LANES), f32),
            pltpu.VMEM((3, cells, LANES), f32),
            pltpu.VMEM((bins, LANES), f32),
            pltpu.VMEM((bins, LANES), f32),
            pltpu.VMEM((bins, LANES), f32),
            pltpu.VMEM((3, ghosts, LANES), f32),
            pltpu.VMEM((4, 8, 3 * slots, LANES), f32),
            pltpu.VMEM((4, 8, 3 * slots, LANES), f32),
            pltpu.VMEM((4, sky_count * depth_count, 1, LANES), f32),
            pltpu.VMEM((LANES // 2 - 1, FIELDS, cells, LANES), f32),
            pltpu.VMEM((LANES, FIELDS, ghosts, LANES), f32),
            dma((4, 8)),
            dma((4, 8)),
            dma((4,)),
            dma((4,)),
        ],
        compiler_params=pltpu.CompilerParams(collective_id=0, has_side_effects=True, vmem_limit_bytes=40 * 1024 * 1024),
        name="descent",
    )(
        positions,
        cell_points,
        target_log,
        export_count,
        jnp.transpose(export_cell, (2, 0, 1)),
        jnp.transpose(import_pair, (2, 0, 1)),
        jnp.transpose(import_shift, (0, 3, 1, 2)),
    )


def solution(mesh):
    in_specs = (
        P(None, ("sky", "depth"), None),
        P(("sky", "depth")),
        P(),
        P(("sky", "depth"), None),
        P(("sky", "depth"), None, None),
        P(("sky", "depth"), None, None),
        P(None, ("sky", "depth"), None, None),
    )
    out_specs = P(None, ("sky", "depth"), None)
    run = functools.partial(body, mesh.shape["sky"], mesh.shape["depth"])
    return jax.shard_map(run, mesh=mesh, in_specs=in_specs, out_specs=out_specs, check_vma=False)
```
